32 devices in a mesh: row: 8 (over z, y), col: 4 (over x, core).
Axes of the slice: x: 2, y: 2, z: 4, core: 2. Of those that a mesh axis runs over, the one named last changes fastest.
Arguments:
- covariance: float32 [12288, 12288], P('row', 'col'), may hold values from -6 to 6
- blocks: float32 [48, 5, 256, 256], P('col', None, 'row'), may hold values from -0.15625 to 0.15625
- present: int32 [48, 5], replicated, may hold values 0 or 1
- model_noise: float32 [12288, 12288], P('col', 'row'), may hold values from -6 to 6
Outputs:
- forecast: float32 [12288, 12288], P('col', 'row')
The draws below stay inside these ranges and needn't reach their ends.
All inputs are finite; a program needn't handle non-finite values.
Results may differ from the reference program's by a relative error of at most 0.000057.
Values sent between devices are 32-bit elements; how exact they have to be, the bound alone decides.
No kernel may reach another device: no remote copies, remote signals or barrier semaphores. Data moves between devices by JAX's collectives and lax.ppermute only.
A program may use at most 320 MiB of HBM per device.

```python
import jax
import jax.numpy as jnp
from jax import lax

N = 12288
BS = 256
NB = 48


def place_ends(values, key, smallest, high):
    longest = values.shape.index(max(values.shape))
    spots = []
    for shift in (0, 1):
        where = [jax.random.randint(jax.random.fold_in(key, axis), (), 0, length) for axis, length in enumerate(values.shape)]
        where[longest] = (where[longest] + shift) % values.shape[longest]
        spots.append(tuple(where))
    return values.at[spots[0]].set(smallest).at[spots[1]].set(high)


def level_of(rng, dims, shards, least, high):
    gain = 1.0
    for dim, parts in shards:
        heights = jax.random.uniform(jax.random.fold_in(jax.random.fold_in(rng, 6), dim), (parts,), jnp.float32, least / len(shards), high / len(shards))
        gain = gain * jnp.repeat(jnp.exp(heights), dims[dim] // parts).reshape((-1,) + (1,) * (len(dims) - 1 - dim))
    return gain


def noise(key, extent, spread, most, pieces=(), kind=jnp.bfloat16):
    array = spread * jax.random.normal(key, extent, jnp.float32)
    if pieces:
        array = array * level_of(key, extent, pieces, -0.22, 0.18)
    return jnp.clip(array, -most, most).astype(kind)


def setup_inputs(seed: int = 0) -> dict:
    seeds = jax.random.split(jax.random.key(seed), 5)
    covariance = noise(seeds[0], (N, N), 1.0, 6.0, ((0, 8), (1, 4)), jnp.float32)
    blocks = noise(seeds[1], (NB, 5, BS, BS), (5 * BS) ** -0.5, 0.15625, ((0, 4), (2, 8)), jnp.float32)
    present = place_ends((jax.random.randint(seeds[2], (NB, 5), 0, 4) < 3).astype(jnp.int32), jax.random.fold_in(seeds[2], 1), 0, 1)
    model_noise = noise(seeds[3], (N, N), 1.0, 6.0, ((0, 4), (1, 8)), jnp.float32)
    return {"covariance": covariance, "blocks": blocks, "present": present, "model_noise": model_noise}


def band_product(live_band, field):
    block_size = live_band.shape[2]
    padded = jnp.pad(field, ((2 * block_size, 2 * block_size), (0, 0)))

    def one_row(pair_item):
        band_row, start = pair_item
        window = lax.dynamic_slice_in_dim(padded, start, 5 * block_size, 0)
        flat_row = jnp.transpose(band_row, (1, 0, 2)).reshape(block_size, 5 * block_size)
        return jnp.dot(flat_row, window, precision=lax.Precision.HIGHEST, preferred_element_type=jnp.float32)

    starts = (jnp.arange(live_band.shape[0]) * block_size).astype(jnp.int32)
    stacked = lax.map(one_row, (live_band, starts))
    return stacked.reshape(-1, field.shape[1])


def reference(covariance, blocks, present, model_noise):
    live_band = blocks * present[:, :, None, None].astype(blocks.dtype)
    mapped = band_product(live_band, covariance)
    return band_product(live_band, mapped.T) + model_noise
```

```python
import functools

import jax
import jax.numpy as jnp
from jax import lax
from jax.experimental import pallas as pl
from jax.experimental.pallas import tpu as pltpu
from jax.sharding import PartitionSpec as P

F32 = jnp.float32
BF16 = jnp.bfloat16
BS = 256
MARGIN = 2 * BS
WIDE = 5 * BS
N = MARGIN
VMEM_BYTES = 56 * 2**20


def after(values, others):
    return lax.optimization_barrier((tuple(values), tuple(others)))[0]


def call(kernel, name, prefetch, grid, in_specs, out_specs, out_shape, scratch, args, flops, alias=None):
    moved = sum(a.size * a.dtype.itemsize for a in args) // 2
    return pl.pallas_call(
        kernel,
        grid_spec=pltpu.PrefetchScalarGridSpec(
            num_scalar_prefetch=len(prefetch), grid=grid, in_specs=in_specs, out_specs=out_specs, scratch_shapes=scratch
        ),
        out_shape=out_shape,
        input_output_aliases=alias or {},
        compiler_params=pltpu.CompilerParams(vmem_limit_bytes=VMEM_BYTES),
        cost_estimate=pl.CostEstimate(flops=flops, bytes_accessed=moved, transcendentals=0),
        name=name,
    )(*prefetch, *args)


def split_into(high_ref, low_ref, rows, value):
    high = value.astype(BF16)
    high_ref[rows, :] = high
    low_ref[rows, :] = (value - high.astype(F32)).astype(BF16)


def dot3(a_high, a_low, b_high, b_low):
    dot = functools.partial(jnp.dot, preferred_element_type=F32)
    return dot(a_high, b_high) + (dot(a_high, b_low) + dot(a_low, b_high))


def place_kernel(count, use, source, first, flags, *refs):
    pieces, outs = refs[:count], refs[count:]
    block = pl.program_id(0)
    slab = pieces[0].shape[3]

    for i, piece in enumerate(pieces):

        @pl.when(use[i] != 0)
        def _(i=i, piece=piece):
            for slot in range(2):
                side = first[i] if slot == 0 else 1 - first[i]
                rows = pl.ds(pl.multiple_of((source[i] * 2 + side) * slab, slab), slab)
                for d in range(5):
                    value = piece[slot, 0, d]
                    columns = pl.ds(d * BS, BS)
                    live = value * flags[block * 5 + d].astype(F32)
                    high = live.astype(BF16)
                    outs[0][0, rows, columns] = high
                    outs[1][0, rows, columns] = (live - high.astype(F32)).astype(BF16)


def place(candidates, flags):
    pieces = [a for a, _, _, _ in candidates]
    table = [jnp.stack([jnp.asarray(c[k], jnp.int32) for c in candidates]) for k in (1, 2, 3)]
    _, blocks, _, slab, _ = pieces[0].shape

    def spec(i):
        return pl.BlockSpec((2, 1, 5, slab, BS), lambda b, use, *_: (0, b * use[i], 0, 0, 0))

    out = pl.BlockSpec((1, BS, WIDE), lambda b, *_: (b, 0, 0))
    return call(
        functools.partial(place_kernel, len(pieces)), "place_slabs", table + [flags], (blocks,),
        [spec(i) for i in range(len(pieces))], [out] * 2,
        [jax.ShapeDtypeStruct((blocks, BS, WIDE), BF16)] * 2, [], pieces, 0,
    )


def inner_kernel(count, y, own, *refs):
    nears, (high_a, low_a, high_b, low_b, out, b_high, b_low) = refs[:count], refs[count:]
    step = pl.program_id(0)
    rows = own.shape[0]
    split_into(b_high, b_low, pl.ds(pl.multiple_of(y[0] * MARGIN, MARGIN), rows), own[...])
    at = pl.ds(pl.multiple_of((1 - y[0]) * rows, MARGIN), MARGIN)
    for i, near in enumerate(nears):

        @pl.when(step == i)
        def _(near=near):
            split_into(b_high, b_low, at, near[...])

    for j in range(4):
        high, low = (high_a, low_a) if j < 2 else (high_b, low_b)
        window = pl.ds(j * BS, WIDE)
        out[:, j * BS : (j + 1) * BS] = dot3(high[j % 2], low[j % 2], b_high[window, :], b_low[window, :]).T


def map_inner(y, covariance, nears, row_high, row_low):
    rows, columns = covariance.shape
    pair_a = pl.BlockSpec((2, BS, WIDE), lambda s, y: (1 - y[0], 0, 0))
    pair_b = pl.BlockSpec((2, BS, WIDE), lambda s, y: (2 - y[0], 0, 0))
    return call(
        functools.partial(inner_kernel, len(nears)), "map_inner", [y], (columns // N,),
        [pl.BlockSpec((rows, N), lambda s, y: (0, s))]
        + [pl.BlockSpec((MARGIN, N), lambda s, y: (0, 0))] * len(nears)
        + [pair_a, pair_a, pair_b, pair_b],
        pl.BlockSpec((N, 4 * BS), lambda s, y: (s + 1, 0)),
        jax.ShapeDtypeStruct((columns + 2 * MARGIN, 4 * BS), F32),
        [pltpu.VMEM((rows + MARGIN, N), BF16)] * 2,
        [covariance, *nears, row_high, row_low, row_high, row_low], 6 * 4 * BS * WIDE * columns,
    )


def outer_kernel(y, own_a, own_b, far, high, low, out, b_high, b_low):
    at = lambda k: pl.ds(pl.multiple_of(k * MARGIN, MARGIN), MARGIN)
    split_into(b_high, b_low, at(1 - y[0]), own_a[...])
    split_into(b_high, b_low, at(2 - y[0]), own_b[...])
    split_into(b_high, b_low, at(2 * y[0]), far[...])
    for j in range(2):
        window = pl.ds(j * BS, WIDE)
        out[:, j * BS : (j + 1) * BS] = dot3(high[j], low[j], b_high[window, :], b_low[window, :]).T


def map_outer(y, covariance, far, row_high, row_low, chunk):
    pair = pl.BlockSpec((2, BS, WIDE), lambda s, y: (2 * y[0], 0, 0))
    return call(
        outer_kernel, "map_outer", [y], (1,),
        [
            pl.BlockSpec((MARGIN, N), lambda s, y: (y[0], chunk)),
            pl.BlockSpec((MARGIN, N), lambda s, y: (y[0] + 1, chunk)),
            pl.BlockSpec((MARGIN, N), lambda s, y: (0, 0)),
            pair, pair,
        ],
        pl.BlockSpec((N, 2 * BS), lambda s, y: (0, 0)),
        jax.ShapeDtypeStruct((N, 2 * BS), F32),
        [pltpu.VMEM((3 * MARGIN, N), BF16)] * 2,
        [covariance, covariance, far, row_high, row_low], 6 * 2 * BS * WIDE * N,
    )


def cast_inner_kernel(aliased, table, padded, high, low, noise, *rest):
    out, b_high, b_low = rest[aliased:]
    step = pl.program_id(0)
    split_into(b_high, b_low, pl.ds(pl.multiple_of(step * BS, BS), BS), padded[...])

    @pl.when(step >= 4)
    def _():
        window = pl.ds(pl.multiple_of((step - 4) * BS, BS), WIDE)
        out[...] = noise[...] + dot3(high[0], low[0], b_high[window, :], b_low[window, :])


def cast_inner(table, padded, high, low, noise, forecast):
    blocks, width = high.shape[0], padded.shape[1]
    row = lambda s: jnp.maximum(s - 4, 0)
    place = pl.BlockSpec(
        (pl.Element(BS), pl.Element(width)), lambda s, t: (pl.multiple_of((t[0] + row(s)) * BS, BS), pl.multiple_of(t[1], N))
    )
    band = pl.BlockSpec((1, BS, WIDE), lambda s, t: (row(s), 0, 0))
    aliased = forecast is not None
    return call(
        functools.partial(cast_inner_kernel, int(aliased)), "cast_inner", [table], (blocks + 4,),
        [pl.BlockSpec((BS, width), lambda s, t: (t[0] + s, 0)), band, band, place]
        + [pl.BlockSpec(memory_space=pl.ANY)] * aliased,
        place, jax.ShapeDtypeStruct(noise.shape, F32), [pltpu.VMEM(((blocks + 4) * BS, width), BF16)] * 2,
        [padded, high, low, noise] + [forecast] * aliased, 6 * blocks * BS * WIDE * width,
        {5: 0} if aliased else None,
    )


def cast_outer_kernel(count, table, *refs):
    parts, (high_a, low_a, high_b, low_b, noise, _, out, b_high, b_low) = refs[:count], refs[count:]
    step = pl.program_id(0)

    @pl.when(step == 0)
    def _():
        for i, part in enumerate(parts):
            split_into(b_high, b_low, pl.ds(i * MARGIN, MARGIN), part[...])

    window = pl.ds(pl.multiple_of(table[step, 1] * BS, BS), WIDE)

    @pl.when(table[step, 2] == 0)
    def _():
        out[...] = noise[...] + dot3(high_a[0], low_a[0], b_high[window, :], b_low[window, :])

    @pl.when(table[step, 2] != 0)
    def _():
        out[...] = noise[...] + dot3(high_b[0], low_b[0], b_high[window, :], b_low[window, :])


def cast_outer(y, rows, starts, parts, bands, noise, forecast):
    blocks = bands[0][0].shape[0]
    table = jnp.array([[row, start, row // blocks, row % blocks] for row, start in zip(rows, starts)], jnp.int32)
    table = table.at[:, 2].set((table[:, 2] + y) % 2)
    column = jnp.broadcast_to(2 * y, (len(rows), 1))
    table = jnp.concatenate([table, column], axis=1)
    place = pl.BlockSpec((BS, N), lambda s, t: (t[s, 0], t[s, 4]))
    band_a = pl.BlockSpec((1, BS, WIDE), lambda s, t: (t[s, 3] * (1 - t[s, 2]), 0, 0))
    band_b = pl.BlockSpec((1, BS, WIDE), lambda s, t: (t[s, 3] * t[s, 2], 0, 0))
    whole = pl.BlockSpec((MARGIN, N), lambda s, t: (0, 0))
    return call(
        functools.partial(cast_outer_kernel, len(parts)), "cast_outer", [table], (len(rows),),
        [whole] * len(parts) + [band_a, band_a, band_b, band_b, place, pl.BlockSpec(memory_space=pl.ANY)],
        place, jax.ShapeDtypeStruct(noise.shape, F32), [pltpu.VMEM((len(parts) * MARGIN, N), BF16)] * 2,
        [*parts, *bands[0], *bands[1], noise, forecast], 6 * len(rows) * BS * WIDE * N, {len(parts) + 6: 0},
    )


def spread(array, axis, root):
    mine = lax.axis_index(axis) == root
    return lax.psum(jnp.where(mine, array, jnp.zeros_like(array)), axis)


def padded_2(cells, sides, width):
    for axis, dim in sides:
        count = lax.axis_size(axis)
        ends = count - 1
        head = lax.slice_in_dim(cells, 0, width, axis=dim)
        tail = lax.slice_in_dim(cells, cells.shape[dim] - width, cells.shape[dim], axis=dim)
        cells = jnp.concatenate(
            [
                lax.ppermute(tail, axis, [(i, (i + 1) % count) for i in range(ends)]),
                cells,
                lax.ppermute(head, axis, [((i + 1) % count, i) for i in range(ends)]),
            ],
            axis=dim,
        )
    return cells


def band_apply(live_band, padded):
    blocks_here = live_band.shape[0]
    block_size = live_band.shape[2]
    columns = padded.shape[1]
    summed = None
    for diagonal in range(5):
        window = padded[diagonal * block_size : (diagonal + blocks_here) * block_size].reshape(
            blocks_here, block_size, columns
        )
        term = jnp.einsum(
            "bij,bjw->biw",
            live_band[:, diagonal],
            window,
            precision=lax.Precision.HIGHEST,
            preferred_element_type=jnp.float32,
        )
        summed = term if summed is None else summed + term
    return summed.reshape(blocks_here * block_size, columns)


def banded(live_band, field, halo_fn):
    return band_apply(live_band, halo_fn(field))


def plain_body(covariance, blocks, present, model_noise):
    row_index = lax.axis_index("row")
    col_index = lax.axis_index("col")
    ratio = lax.axis_size("row") // lax.axis_size("col")
    column_band = lax.all_gather(blocks, "row", axis=2, tiled=True)
    col_blocks = column_band.shape[0]
    row_blocks = col_blocks // ratio
    own_part = lax.dynamic_slice_in_dim(column_band, row_index % ratio * row_blocks, row_blocks, 0)
    row_band = spread(own_part, "col", row_index // ratio)
    flags = present.astype(jnp.float32)
    col_flags = lax.dynamic_slice_in_dim(flags, col_index * col_blocks, col_blocks, 0)
    row_flags = lax.dynamic_slice_in_dim(flags, row_index * row_blocks, row_blocks, 0)
    live_col = column_band * col_flags[:, :, None, None]
    live_row = row_band * row_flags[:, :, None, None]
    margin = 2 * blocks.shape[3]

    def row_margin(field):
        return padded_2(field, (("row", 0),), margin)

    def col_margin(field):
        return padded_2(field, (("col", 0),), margin)

    mapped = banded(live_row, covariance, row_margin)
    second = banded(live_col, mapped.T, col_margin)
    return second + model_noise


def body(covariance, blocks, present, model_noise):
    rows, cols = lax.axis_size("row"), lax.axis_size("col")
    r, c = lax.axis_index("row"), lax.axis_index("col")
    z, y = r // 2, r % 2
    depth = rows // 2
    col_blocks, _, slab, _ = blocks.shape
    part_blocks = col_blocks // 2
    swap = [(i, i ^ 1) for i in range(rows)]
    permute = lax.ppermute
    y_table = jnp.reshape(y, (1,)).astype(jnp.int32)

    sliced = blocks.reshape(2, part_blocks, 5, slab, BS)
    pick = lambda part: lax.dynamic_index_in_dim(sliced, part % 2, 0, False)

    def along(k, long, ends=True):
        hops = []
        for i in range(k - 1, depth - 1):
            hops.append((2 * i, 2 * i + 2) if long else (2 * i + 1, 2 * i + 3))
        for i in range(0, depth - k):
            hops.append((2 * i + 3, 2 * i + 1) if long else (2 * i + 2, 2 * i))
        return [(a, b) for a, b in hops if ends or b not in (0, rows - 1)]

    home = r // 2
    bits = [1 << b for b in reversed(range(cols.bit_length() - 1))]

    def senders(missing, bit, keep):
        pairs_of = [(i, a) for i in range(rows) if keep(i) for a in range(cols) if ((a ^ (i // 2)) & missing) == 0]
        return [(i * cols + a, i * cols + (a ^ bit)) for i, a in pairs_of]

    def keeps(k, long):
        def keep(i):
            up = (i % 2 == 0) == long
            return i // 2 >= k if up else i // 2 + k < depth

        return keep

    axes = ("row", "col")
    at_home, at_mate = c == home, c == home ^ bits[0]

    extra = covariance.shape[0] - MARGIN
    count = covariance.shape[1] // N
    chunks = sorted(range(count), key=lambda s: min(s, count - 1 - s))
    hops = [(i, i + 1) for i in range(1, rows - 1, 2)] + [(i + 1, i) for i in range(1, rows - 1, 2)]
    near_parts = [(lax.dynamic_slice(covariance, (extra * (1 - y), i * N), (MARGIN, N)), "row", swap) for i in range(count)]
    far_parts = [(lax.dynamic_slice(covariance, (extra * y, i * N), (MARGIN, N)), "row", hops) for i in chunks]

    def send(jobs, *others):
        values = after([job[0] for job in jobs], others)
        return [permute(value, axis, perm) for value, (_, axis, perm) in zip(values, jobs)]

    trips = near_parts + far_parts
    long0, short0, long1, short1 = ([] for _ in range(4))
    passed = {}
    trades = [permute(pick(1 - y), "row", swap)]
    pair0 = jnp.stack([pick(y), trades[0]])
    long0.append(pair0)
    short0.append(pair0)
    over = [None]

    def relays(k):
        jobs = [(long0[k], axes, senders(cols - 1, bits[0], keeps(k, True)))]
        return jobs if k == 0 else jobs + [(short0[k], axes, senders(cols - 1, bits[0], keeps(k, False)))]

    def climbed(k, up):
        return jnp.where(up, z >= k, z + k < depth), jnp.where(up, z - k, z + k)

    def entry(value, k, up, when, first=y):
        held, source = climbed(k, up)
        return value, held & when, jnp.clip(source, 0, depth - 1), first

    end = ((y == 0) & (z == 0)) | ((y == 1) & (z == depth - 1))
    always = z >= 0
    row_flags = lax.dynamic_slice_in_dim(present, r * part_blocks, part_blocks, 0).reshape(-1)

    def place_rows():
        table = []
        for k in range(depth):
            for i, (long, value) in enumerate(((True, long0[k]), (False, short0[k]))):
                if k == 0 and not long:
                    continue
                up = (y == 0) if long else (y == 1)
                got = passed[k, i][0]
                pairs_of = senders(cols - 1 - bits[0], bits[1], keeps(k, long))
                beside = permute(jnp.where(at_mate, got, value), axes, pairs_of)
                table += [entry(value, k, up, at_home), entry(got, k, up, at_mate), entry(beside, k, up, ~(at_home | at_mate))]
        return place(table, row_flags)

    def place_columns(phase):
        table = [entry((pair0, pair1)[phase], 0, True, always)]
        for k in range(1, depth):
            if phase == 0:
                table += [entry(long0[k], k, y == 0, always), entry(short0[k], k, y == 1, always)]
            else:
                table += [entry(long1[k], k, y == 0, always), entry(over[k], k, y == 1, end, 1 - y)]
                if k < depth - 1:
                    table.append(entry(short1[k], k, y == 1, ~end))
        base = c * col_blocks + (y + phase) % 2 * part_blocks
        return place(table, lax.dynamic_slice_in_dim(present, base, part_blocks, 0).reshape(-1))

    def inner_table(phase):
        return jnp.stack([(y + phase) % 2 * part_blocks, (1 - y) * N]).astype(jnp.int32)

    def arrived(i):
        return even[(i + 1) // 2] if i % 2 else odd[i // 2]

    up, down = [(i, i + 1) for i in range(cols - 1)], [(i + 1, i) for i in range(cols - 1)]
    mapped = {}
    even, odd, stage = [], [], [trades[0]]
    for s in range(1, count + 2):
        jobs, sinks = [(pick(1 - y + 1), "row", swap) if s == 1 else trips[2 * s - 3]], [even]
        if s < depth:
            jobs += [(long0[s - 1], "row", along(s, True)), (short0[s - 1], "row", along(s, False))]
            sinks += [long0, short0]
        if s == depth - 1 or s == depth:
            k = s - depth + 2
            if k == 1:
                short1.append(pair1)
            jobs.append((short1[k - 1], "row", along(k, False, False)))
            sinks.append(short1)
        if depth <= s < 2 * depth - 1:
            k = s - depth + 1
            if k == 1:
                long1.append(pair1)
            jobs.append((long1[k - 1], "row", along(k, True)))
            sinks.append(long1)
        if depth < s < 2 * depth:
            jobs.append((long0[s - depth], "row", [(1, 0), (rows - 2, rows - 1)]))
            sinks.append(over)
        if s <= depth:
            jobs += relays(s - 1)
            sinks += [passed.setdefault((s - 1, i), []) for i in range(1 if s == 1 else 2)]
        results = send(jobs, *stage, *odd[-2:-1])
        if 2 * s - 2 < len(trips):
            odd += send([trips[2 * s - 2]], *stage, *odd[-1:])
        for sink, result in zip(sinks, results):
            sink.append(result)
        stage = results
        if s == 1:
            pair1 = jnp.stack([pick(y + 1), even[0]])
        if s == depth:
            bands = [place_columns(0)]
            row_high, row_low = place_rows()
            stage = stage + [bands[0][0], row_high]
        if s == depth + 1:
            nears = [arrived(i) for i in range(count)]
            padded = map_inner(y_table, covariance, nears, row_high, row_low)
            stage = stage + [padded]
        if s > depth + 1:
            for i in range(2 * (s - depth - 2), 2 * (s - depth - 1)):
                mapped[chunks[i]] = map_outer(y_table, covariance, arrived(count + i), row_high, row_low, chunks[i])
                stage = stage + [mapped[chunks[i]]]
        if s == depth + 2:
            end_row = padded.shape[0] - MARGIN
            below = permute(padded[end_row - MARGIN : end_row], "col", up)
            above = permute(padded[MARGIN : 2 * MARGIN], "col", down)
            padded = lax.dynamic_update_slice(padded, below, (0, 0))
            padded = lax.dynamic_update_slice(padded, above, (end_row, 0))
            mapped[-1] = permute(mapped[count - 1], "col", up)
            mapped[count] = permute(mapped[0], "col", down)
            forecast = cast_inner(inner_table(0), padded, *bands[0], model_noise, None)
            stage = stage + [forecast]
    for i in range(count - 2, count):
        mapped[chunks[i]] = map_outer(y_table, covariance, arrived(count + i), row_high, row_low, chunks[i])
    bands.append(place_columns(1))

    forecast = cast_inner(inner_table(1), padded, *bands[1], model_noise, forecast)
    late = chunks[-1]
    tail_rows = range(2 * late - 2, 2 * late + 4)
    tail_parts = range(late - 2, late + 3)
    last = count - 1
    head_rows = [b for b in range(col_blocks) if b not in tail_rows]
    head_parts = [p for p in range(-1, last + 2) if p != late]
    spot = {2 * p + i: 2 * k + i for k, p in enumerate(head_parts) for i in range(2)}
    forecast = cast_outer(y, head_rows, [spot[b - 2] for b in head_rows], [mapped[p] for p in head_parts], bands, model_noise, forecast)
    return cast_outer(y, tail_rows, range(6), [mapped[p] for p in tail_parts], bands, model_noise, forecast)


def solution(mesh):
    rows, cols = mesh.shape["row"], mesh.shape["col"]
    in_specs = (P("row", "col"), P("col", None, "row", None), P(), P("col", "row"))

    def step(covariance, blocks, present, model_noise):
        fits = rows == 2 * cols and rows == 8 and blocks.shape[0] == 12 * cols
        chosen = body if fits and blocks.shape[3] == BS else plain_body
        inner = jax.shard_map(chosen, mesh=mesh, in_specs=in_specs, out_specs=P("col", "row"), check_vma=False)
        return inner(covariance, blocks, present, model_noise)

    return step
```

```python
import functools
import itertools

import jax
import jax.numpy as jnp
from jax import lax
from jax.experimental import pallas as pl
from jax.experimental.pallas import tpu as pltpu
from jax.sharding import PartitionSpec as P

F32 = jnp.float32
BF16 = jnp.bfloat16
BS = 256
MARGIN = 2 * BS
WIDE = 5 * BS
N = MARGIN
PLACED = 1
VMEM_BYTES = 56 * 2**20


def after(values, others):
    return lax.optimization_barrier((tuple(values), tuple(others)))[0]


def call(kernel, name, prefetch, grid, in_specs, out_specs, out_shape, scratch, args, flops, alias=None):
    moved = sum(a.size * a.dtype.itemsize for a in args) // 2
    return pl.pallas_call(
        kernel,
        grid_spec=pltpu.PrefetchScalarGridSpec(
            num_scalar_prefetch=len(prefetch), grid=grid, in_specs=in_specs, out_specs=out_specs, scratch_shapes=scratch
        ),
        out_shape=out_shape,
        input_output_aliases=alias or {},
        compiler_params=pltpu.CompilerParams(vmem_limit_bytes=VMEM_BYTES),
        cost_estimate=pl.CostEstimate(flops=flops, bytes_accessed=moved, transcendentals=0),
        name=name,
    )(*prefetch, *args)


def split_into(high_ref, low_ref, rows, value):
    high = value.astype(BF16)
    high_ref[rows, :] = high
    low_ref[rows, :] = (value - high.astype(F32)).astype(BF16)


def dot3(a_high, a_low, b_high, b_low):
    dot = functools.partial(jnp.dot, preferred_element_type=F32)
    return dot(a_high, b_high) + (dot(a_high, b_low) + dot(a_low, b_high))


def place_kernel(count, use, source, first, flags, *refs):
    pieces, outs = refs[:count], refs[count:]
    block = pl.program_id(0) * PLACED
    slab = pieces[0].shape[3]

    for i, piece in enumerate(pieces):

        @pl.when(use[i] != 0)
        def _(i=i, piece=piece):
            for slot in range(2):
                side = first[i] if slot == 0 else 1 - first[i]
                rows = pl.ds(pl.multiple_of((source[i] * 2 + side) * slab, slab), slab)
                for b, d in itertools.product(range(PLACED), range(5)):
                    columns = pl.ds(d * BS, BS)
                    live = piece[slot, b, d] * flags[(block + b) * 5 + d].astype(F32)
                    high = live.astype(BF16)
                    outs[0][b, rows, columns] = high
                    outs[1][b, rows, columns] = (live - high.astype(F32)).astype(BF16)


def place(candidates, flags):
    pieces = [a for (a, _), _, _, _ in candidates]
    table = [jnp.stack([jnp.asarray(c[k], jnp.int32) for c in candidates]) for k in (1, 2, 3)]
    _, blocks, _, slab, _ = pieces[0].shape

    def spec(i):
        pair = candidates[i][0][1]
        return pl.BlockSpec((2, PLACED, 5, slab, BS), lambda b, use, *_: (pair, b * use[i], 0, 0, 0))

    out = pl.BlockSpec((PLACED, BS, WIDE), lambda b, *_: (b, 0, 0))
    return call(
        functools.partial(place_kernel, len(pieces)), "place_slabs", table + [flags], (blocks // PLACED,),
        [spec(i) for i in range(len(pieces))], [out] * 2,
        [jax.ShapeDtypeStruct((blocks, BS, WIDE), BF16)] * 2, [], pieces, 0,
    )


def inner_kernel(count, y, own, *refs):
    nears, (high_a, low_a, high_b, low_b, out, head, tail, b_high, b_low) = refs[:count], refs[count:]
    step = pl.program_id(0)
    rows = own.shape[0]
    split_into(b_high, b_low, pl.ds(pl.multiple_of(y[0] * MARGIN, MARGIN), rows), own[...])
    at = pl.ds(pl.multiple_of((1 - y[0]) * rows, MARGIN), MARGIN)
    for i, near in enumerate(nears):

        @pl.when(step == i)
        def _(near=near):
            split_into(b_high, b_low, at, near[...])

    for j in range(4):
        high, low = (high_a, low_a) if j < 2 else (high_b, low_b)
        window = pl.ds(j * BS, WIDE)
        out[:, j * BS : (j + 1) * BS] = dot3(high[j % 2], low[j % 2], b_high[window, :], b_low[window, :]).T

    @pl.when(step == 0)
    def _():
        head[...] = out[...]

    @pl.when(step == count - 1)
    def _():
        tail[...] = out[...]


def map_inner(y, covariance, nears, row_high, row_low):
    rows, columns = covariance.shape
    pair_a = pl.BlockSpec((2, BS, WIDE), lambda s, y: (1 - y[0], 0, 0))
    pair_b = pl.BlockSpec((2, BS, WIDE), lambda s, y: (2 - y[0], 0, 0))
    edge = pl.BlockSpec((N, 4 * BS), lambda s, y: (0, 0))
    return call(
        functools.partial(inner_kernel, len(nears)), "map_inner", [y], (columns // N,),
        [pl.BlockSpec((rows, N), lambda s, y: (0, s))]
        + [pl.BlockSpec((MARGIN, N), lambda s, y, at=at: (0, at)) for _, at in nears]
        + [pair_a, pair_a, pair_b, pair_b],
        [pl.BlockSpec((N, 4 * BS), lambda s, y: (s, 0)), edge, edge],
        [jax.ShapeDtypeStruct((columns, 4 * BS), F32)] + [jax.ShapeDtypeStruct((N, 4 * BS), F32)] * 2,
        [pltpu.VMEM((rows + MARGIN, N), BF16)] * 2,
        [covariance, *[near for near, _ in nears], row_high, row_low, row_high, row_low], 6 * 4 * BS * WIDE * columns,
    )


def outer_kernel(count, y, chunks, own_a, own_b, *refs):
    fars, (high, low), outs, (b_high, b_low) = refs[:count], refs[count : count + 2], refs[count + 2 : -2], refs[-2:]
    at = lambda k: pl.ds(pl.multiple_of(k * MARGIN, MARGIN), MARGIN)
    split_into(b_high, b_low, at(1 - y[0]), own_a[...])
    split_into(b_high, b_low, at(2 - y[0]), own_b[...])
    for i, far in enumerate(fars):

        @pl.when(pl.program_id(0) == i)
        def _(far=far):
            split_into(b_high, b_low, at(2 * y[0]), far[...])

    for j in range(2):
        window = pl.ds(j * BS, WIDE)
        mapped = dot3(high[j], low[j], b_high[window, :], b_low[window, :]).T
        for i, out in enumerate(outs):

            @pl.when(pl.program_id(0) == i)
            def _(out=out):
                out[:, j * BS : (j + 1) * BS] = mapped


def map_outer(y, covariance, fars, row_high, row_low, chunks):
    pair = pl.BlockSpec((2, BS, WIDE), lambda s, y, c: (2 * y[0], 0, 0))
    return call(
        functools.partial(outer_kernel, len(fars)), "map_outer", [y, jnp.array(chunks, jnp.int32)], (len(chunks),),
        [
            pl.BlockSpec((MARGIN, N), lambda s, y, c: (y[0], c[s])),
            pl.BlockSpec((MARGIN, N), lambda s, y, c: (y[0] + 1, c[s])),
        ]
        + [pl.BlockSpec((MARGIN, N), lambda s, y, c, at=at: (0, at)) for _, at in fars]
        + [pair, pair],
        [pl.BlockSpec((N, 2 * BS), lambda s, y, c: (0, 0))] * len(chunks),
        [jax.ShapeDtypeStruct((N, 2 * BS), F32)] * len(chunks),
        [pltpu.VMEM((3 * MARGIN, N), BF16)] * 2,
        [covariance, covariance, *[far for far, _ in fars], row_high, row_low], 6 * 2 * BS * WIDE * N * len(chunks),
    )


def split_next(count, at, parts, high_ref, low_ref):
    rows = pl.ds(pl.multiple_of(pl.program_id(0) * BS, BS), BS)
    for part, here in zip(parts, (at < 2, (at >= 2) & (at < count + 2), at >= count + 2)):

        @pl.when(here)
        def _(part=part):
            split_into(high_ref, low_ref, rows, part[...])


def streams(count, width):
    def spec(first, blocks):
        return pl.BlockSpec((BS, width), lambda s, t: (jnp.clip(t[0] + s - first, 0, blocks - 1), 0))

    return [spec(0, 2), spec(2, count), spec(count + 2, 2)]


def cast_inner_kernel(count, aliased, table, below, mid, above, high, low, noise, *rest):
    out, b_high, b_low = rest[aliased:]
    step = pl.program_id(0)
    split_next(count, table[0] + step, (below, mid, above), b_high, b_low)

    @pl.when(step >= 4)
    def _():
        window = pl.ds(pl.multiple_of((step - 4) * BS, BS), WIDE)
        out[...] = noise[...] + dot3(high[0], low[0], b_high[window, :], b_low[window, :])


def cast_inner(table, padded, high, low, noise, forecast):
    blocks, (length, width) = high.shape[0], padded[1].shape
    row = lambda s: jnp.maximum(s - 4, 0)
    place = pl.BlockSpec(
        (pl.Element(BS), pl.Element(width)), lambda s, t: (pl.multiple_of((t[0] + row(s)) * BS, BS), pl.multiple_of(t[1], N))
    )
    band = pl.BlockSpec((1, BS, WIDE), lambda s, t: (row(s), 0, 0))
    aliased = forecast is not None
    return call(
        functools.partial(cast_inner_kernel, length // BS, int(aliased)), "cast_inner", [table], (blocks + 4,),
        [*streams(length // BS, width), band, band, place]
        + [pl.BlockSpec(memory_space=pl.ANY)] * aliased,
        place, jax.ShapeDtypeStruct(noise.shape, F32), [pltpu.VMEM(((blocks + 4) * BS, width), BF16)] * 2,
        [*padded, high, low, noise] + [forecast] * aliased, 6 * blocks * BS * WIDE * width,
        {7: 0} if aliased else None,
    )


def cast_outer_kernel(count, held, table, *refs):
    parts, (high, low, noise, _, out, b_high, b_low) = refs[:count], refs[count:]
    step = pl.program_id(0)

    @pl.when(step == 0)
    def _():
        for i, part in enumerate(parts):

            @pl.when((i >= table[1]) & (i < table[1] + held))
            def _(i=i, part=part):
                split_into(b_high, b_low, pl.ds(pl.multiple_of((i - table[1]) * MARGIN, MARGIN), MARGIN), part[...])

    window = pl.ds(pl.multiple_of(step * BS, BS), WIDE)
    out[...] = noise[...] + dot3(high[0], low[0], b_high[window, :], b_low[window, :])


def cast_outer(table, parts, high, low, noise, forecast):
    blocks = high.shape[0]
    held = blocks // 2 + 2
    place = pl.BlockSpec((BS, N), lambda s, t: (t[0] + s, t[2]))
    band = pl.BlockSpec((1, BS, WIDE), lambda s, t: (s, 0, 0))
    return call(
        functools.partial(cast_outer_kernel, len(parts), held), "cast_outer", [table], (blocks,),
        [pl.BlockSpec((MARGIN, N), lambda s, t, at=at: (at, 0)) for _, at in parts]
        + [band, band, place, pl.BlockSpec(memory_space=pl.ANY)],
        place, jax.ShapeDtypeStruct(noise.shape, F32), [pltpu.VMEM((held * MARGIN, N), BF16)] * 2,
        [*[part for part, _ in parts], high, low, noise, forecast], 6 * blocks * BS * WIDE * N, {len(parts) + 4: 0},
    )


def cast_rest_kernel(blocks, count, held, table, below, mid, above, *refs):
    parts, (high, low, noise, _, out, in_high, in_low, out_high, out_low) = refs[:count], refs[count:]
    step = pl.program_id(0)
    split_next(blocks, table[0] + step, (below, mid, above), in_high, in_low)

    @pl.when(step == 0)
    def _():
        for i, part in enumerate(parts):

            @pl.when((i >= table[1]) & (i < table[1] + held))
            def _(i=i, part=part):
                split_into(out_high, out_low, pl.ds(pl.multiple_of((i - table[1]) * MARGIN, MARGIN), MARGIN), part[...])

    @pl.when(step >= 4)
    def _():
        window = pl.ds(pl.multiple_of((step - 4) * BS, BS), WIDE)
        inner = pl.ds(pl.multiple_of(table[2], N), mid.shape[1])
        outer = pl.ds(pl.multiple_of(table[3], N), N)
        out[:, inner] = noise[:, inner] + dot3(high[0], low[0], in_high[window, :], in_low[window, :])
        out[:, outer] = noise[:, outer] + dot3(high[0], low[0], out_high[window, :], out_low[window, :])


def cast_rest(table, padded, parts, high, low, noise, forecast):
    blocks, (length, width) = high.shape[0], padded[1].shape
    held = blocks // 2 + 2
    row = lambda s: jnp.maximum(s - 4, 0)
    place = pl.BlockSpec((BS, noise.shape[1]), lambda s, t: (t[0] + row(s), 0))
    band = pl.BlockSpec((1, BS, WIDE), lambda s, t: (row(s), 0, 0))
    rows = (blocks + 4) * BS
    return call(
        functools.partial(cast_rest_kernel, length // BS, len(parts), held), "cast_rest", [table], (blocks + 4,),
        streams(length // BS, width)
        + [pl.BlockSpec((MARGIN, N), lambda s, t, at=at: (at, 0)) for _, at in parts]
        + [band, band, place, pl.BlockSpec(memory_space=pl.ANY)],
        place, jax.ShapeDtypeStruct(noise.shape, F32),
        [pltpu.VMEM((rows, width), BF16)] * 2 + [pltpu.VMEM((rows, N), BF16)] * 2,
        [*padded, *[part for part, _ in parts], high, low, noise, forecast], 6 * blocks * BS * WIDE * noise.shape[1],
        {len(parts) + 7: 0},
    )


def spread(array, axis, root):
    mine = lax.axis_index(axis) == root
    return lax.psum(jnp.where(mine, array, jnp.zeros_like(array)), axis)


def padded_2(cells, sides, width):
    for axis, dim in sides:
        count = lax.axis_size(axis)
        ends = count - 1
        head = lax.slice_in_dim(cells, 0, width, axis=dim)
        tail = lax.slice_in_dim(cells, cells.shape[dim] - width, cells.shape[dim], axis=dim)
        cells = jnp.concatenate(
            [
                lax.ppermute(tail, axis, [(i, (i + 1) % count) for i in range(ends)]),
                cells,
                lax.ppermute(head, axis, [((i + 1) % count, i) for i in range(ends)]),
            ],
            axis=dim,
        )
    return cells


def band_apply(live_band, padded):
    blocks_here = live_band.shape[0]
    block_size = live_band.shape[2]
    columns = padded.shape[1]
    summed = None
    for diagonal in range(5):
        window = padded[diagonal * block_size : (diagonal + blocks_here) * block_size].reshape(
            blocks_here, block_size, columns
        )
        term = jnp.einsum(
            "bij,bjw->biw",
            live_band[:, diagonal],
            window,
            precision=lax.Precision.HIGHEST,
            preferred_element_type=jnp.float32,
        )
        summed = term if summed is None else summed + term
    return summed.reshape(blocks_here * block_size, columns)


def banded(live_band, field, halo_fn):
    return band_apply(live_band, halo_fn(field))


def plain_body(covariance, blocks, present, model_noise):
    row_index = lax.axis_index("row")
    col_index = lax.axis_index("col")
    ratio = lax.axis_size("row") // lax.axis_size("col")
    column_band = lax.all_gather(blocks, "row", axis=2, tiled=True)
    col_blocks = column_band.shape[0]
    row_blocks = col_blocks // ratio
    own_part = lax.dynamic_slice_in_dim(column_band, row_index % ratio * row_blocks, row_blocks, 0)
    row_band = spread(own_part, "col", row_index // ratio)
    flags = present.astype(jnp.float32)
    col_flags = lax.dynamic_slice_in_dim(flags, col_index * col_blocks, col_blocks, 0)
    row_flags = lax.dynamic_slice_in_dim(flags, row_index * row_blocks, row_blocks, 0)
    live_col = column_band * col_flags[:, :, None, None]
    live_row = row_band * row_flags[:, :, None, None]
    margin = 2 * blocks.shape[3]

    def row_margin(field):
        return padded_2(field, (("row", 0),), margin)

    def col_margin(field):
        return padded_2(field, (("col", 0),), margin)

    mapped = banded(live_row, covariance, row_margin)
    second = banded(live_col, mapped.T, col_margin)
    return second + model_noise


def body(covariance, blocks, present, model_noise):
    rows, cols = lax.axis_size("row"), lax.axis_size("col")
    r, c = lax.axis_index("row"), lax.axis_index("col")
    z, y = r // 2, r % 2
    depth = rows // 2
    col_blocks, _, slab, _ = blocks.shape
    part_blocks = col_blocks // 2
    swap = [(i, i ^ 1) for i in range(rows)]
    permute = lax.ppermute
    y_table = jnp.reshape(y, (1,)).astype(jnp.int32)

    sliced = blocks.reshape(2, part_blocks, 5, slab, BS)
    pick = lambda part: lax.dynamic_index_in_dim(sliced, part % 2, 0, False)

    def along(k, long, ends=True):
        hops = []
        for i in range(k - 1, depth - 1):
            hops.append((2 * i, 2 * i + 2) if long else (2 * i + 1, 2 * i + 3))
        for i in range(0, depth - k):
            hops.append((2 * i + 3, 2 * i + 1) if long else (2 * i + 2, 2 * i))
        return [(a, b) for a, b in hops if ends or b not in (0, rows - 1)]

    home = r // 2
    bits = [1 << b for b in reversed(range(cols.bit_length() - 1))]

    def senders(missing, bit, keep):
        pairs_of = [(i, a) for i in range(rows) if keep(i) for a in range(cols) if ((a ^ (i // 2)) & missing) == 0]
        return [(i * cols + a, i * cols + (a ^ bit)) for i, a in pairs_of]

    def keeps(k, long):
        def keep(i):
            up = (i % 2 == 0) == long
            return i // 2 >= k if up else i // 2 + k < depth

        return keep

    axes = ("row", "col")
    at_home, at_mate = c == home, c == home ^ bits[0]

    extra = covariance.shape[0] - MARGIN
    count = covariance.shape[1] // N
    chunks = sorted(range(count), key=lambda s: min(s, count - 1 - s))
    hops = [(i, i + 1) for i in range(1, rows - 1, 2)] + [(i + 1, i) for i in range(1, rows - 1, 2)]
    spans = [(0, 1), (1, 2), (3, 2), (5, 1)]
    near_trips = [
        (lax.dynamic_slice(covariance, (extra * (1 - y), at * N), (MARGIN, n * N)), "row", swap) for at, n in spans
    ]
    far_spans = [chunks[:1], chunks[1:3], chunks[3:5], chunks[5:]]
    far_trips = []
    for span in far_spans:
        pieces = [lax.dynamic_slice(covariance, (extra * y, i * N), (MARGIN, N)) for i in span]
        far_trips.append((jnp.concatenate(pieces, axis=1), "row", hops))

    def send(jobs, *others):
        values = after([job[0] for job in jobs], others)
        return [permute(value, axis, perm) for value, (_, axis, perm) in zip(values, jobs)]

    def pass_x(k, long):
        return senders(cols - 1, bits[0], keeps(k, long))

    def pass_core(k, long):
        return senders(cols - 1 - bits[0], bits[1], keeps(k, long))

    def join(*lists):
        return [pair for pairs in lists for pair in pairs]

    def whole(hops):
        return [(i * cols + a, j * cols + a) for i, j in hops for a in range(cols)]

    def among(hops):
        return functools.reduce(jnp.logical_or, [r == i for i, _ in hops])

    def core(value, passed, k, long):
        return permute(jnp.where(at_mate, passed, value), axes, pass_core(k, long))

    over = [(1, 0), (rows - 2, rows - 1)]
    ends_hops, inside_hops = along(3, False), along(1, False, False)
    trade0 = permute(pick(1 - y), "row", swap)
    pair0 = jnp.stack([pick(y), trade0])
    main = send(
        [(pick(1 - y + 1), "row", swap), near_trips[0], (pair0, "row", along(1, True)), (pair0, "row", along(1, False))], trade0
    )
    trade1, near0, long01, short01 = main
    (x0,) = send([(pair0, axes, pass_x(0, True))], trade1)
    pair1 = jnp.stack([pick(y + 1), trade1])
    stage = main + [x0] + [value for value, _, _ in near_trips[1:]]
    main = send([near_trips[1], (long01, "row", along(2, True)), (short01, "row", along(2, False))], *stage)
    near1, long02, short02 = main
    x1a, core0 = send(
        [(long01, axes, pass_x(1, True)), (jnp.where(at_mate, x0, pair0), axes, pass_core(0, True))], *stage, pair1
    )
    climbs = lambda k: jnp.where(y == 0, z >= k, z + k < depth)
    stage = main + [x1a, core0] + [value for value, _, _ in far_trips]
    last_hops = along(3, True) + along(3, False)
    value2 = jnp.where(climbs(2), long02, short02)
    near2, ends3, short11, x2, x1b = main = send(
        [
            near_trips[2], (value2, "row", last_hops), (pair1, "row", along(1, False, False)),
            (value2, axes, senders(cols - 1, bits[0], lambda i: True)), (short01, axes, pass_x(1, False)),
        ],
        *stage,
    )
    (core1a,) = send([(jnp.where(at_mate, x1a, long01), axes, pass_core(1, True))], x2)
    stage = main + [core1a]
    inside2 = along(2, False, False)
    x3_keep = lambda i: i // 2 in (0, depth - 1)
    near3, far0, long11, mixed4, core12 = stage = send(
        [
            near_trips[3], far_trips[0], (pair1, "row", along(1, True)),
            (jnp.where(among(inside2), short11, ends3), axes, whole(inside2) + senders(cols - 1, bits[0], x3_keep)),
            (
                jnp.concatenate([jnp.where(at_mate, x1b, short01), jnp.where(at_mate, x2, value2)]),
                axes, senders(cols - 1 - bits[0], bits[1], lambda i: True),
            ),
        ],
        *stage,
    )

    def climbed(k, up):
        return jnp.where(up, z >= k, z + k < depth), jnp.where(up, z - k, z + k)

    def entry(value, k, up, when, first=y):
        held, source = climbed(k, up)
        value = value if isinstance(value, tuple) else (value, 0)
        return value, held & when, jnp.clip(source, 0, depth - 1), first

    def either(value, k, when):
        value, _, below, first = entry(value, k, False, when)
        _, _, above, _ = entry(value, k, True, when)
        held = ((z >= k) | (z + k < depth)) & when
        return value, held, jnp.where(z >= k, above, below), first

    end = ((y == 0) & (z == 0)) | ((y == 1) & (z == depth - 1))
    always = z >= 0
    row_flags = lax.dynamic_slice_in_dim(present, r * part_blocks, part_blocks, 0).reshape(-1)

    def part_flags(phase):
        base = c * col_blocks + (y + phase) % 2 * part_blocks
        return lax.dynamic_slice_in_dim(present, base, part_blocks, 0).reshape(-1)

    longs, shorts = y == 0, y == 1
    at_other = ~(at_home | at_mate)
    columns0 = [
        entry(pair0, 0, True, always), entry(long01, 1, longs, always), entry(short01, 1, shorts, always),
        either(value2, 2, always), either(ends3, 3, always),
    ]
    bands = [place(columns0, part_flags(0))]
    stage = list(stage) + [bands[0][0]]

    def inner_table(phase):
        return jnp.stack([(y + phase) % 2 * part_blocks, (1 - y) * N]).astype(jnp.int32)

    def outer_table(phase):
        half = (y + phase) % 2
        return jnp.stack([half * part_blocks, half * (part_blocks // 2), 2 * y]).astype(jnp.int32)

    def outer(first, number):
        picked = list(range(first, first + number))
        outs = map_outer(y_table, covariance, [fars[i] for i in picked], row_high, row_low, [chunks[i] for i in picked])
        mapped.update((chunks[i], (out, 0)) for i, out in zip(picked, outs))
        return outs

    up, down = [(i, i + 1) for i in range(cols - 1)], [(i + 1, i) for i in range(cols - 1)]
    mapped, fars = {}, [(far0, 0)]
    stage4 = stage
    far12, long12, over1 = stage = send(
        [far_trips[1], (long11, "row", along(2, True)), (long01, "row", over)], *stage
    )
    (core3,) = send(
        [(jnp.where(at_mate, mixed4, ends3), axes, senders(cols - 1 - bits[0], bits[1], x3_keep))], *stage4
    )
    core1b, core2 = (core12, 0), (core12, 1)
    row_table = [entry(pair0, 0, True, at_home), entry(x0, 0, True, at_mate), entry(core0, 0, True, at_other)]
    for k, way, values in (
        (1, longs, (long01, x1a, core1a)), (1, shorts, (short01, x1b, core1b)),
    ):
        row_table += [entry(value, k, way, when) for value, when in zip(values, (at_home, at_mate, at_other))]
    for k, values in ((2, (value2, x2, core2)), (3, (ends3, mixed4, core3))):
        row_table += [either(value, k, when) for value, when in zip(values, (at_home, at_mate, at_other))]
    row_high, row_low = place(row_table, row_flags)
    near_blocks = [(near, i) for near, (_, n) in zip((near0, near1, near2, near3), spans) for i in range(n)]
    inner, inner_head, inner_tail = map_inner(y_table, covariance, near_blocks, row_high, row_low)
    far34, long13, over2, below, above = stage = send(
        [
            far_trips[2], (long12, "row", along(3, True)), (long02, "row", over),
            (inner_tail, "col", up), (inner_head, "col", down),
        ],
        *stage, inner,
    )
    fars += [(far12, 0), (far12, 1), (far34, 0), (far34, 1)]
    first_mapped = outer(0, 3)
    padded = (below, inner, above)
    forecast = cast_inner(inner_table(0), padded, *bands[0], model_noise, None)
    far5, last_over, outer_below, outer_above = send(
        [far_trips[3], (ends3, "row", over), (mapped[count - 1][0], "col", up), (mapped[0][0], "col", down)],
        *stage, *first_mapped, forecast,
    )
    fars.append((far5, 0))
    mapped[-1], mapped[count] = (outer_below, 0), (outer_above, 0)
    outer(3, 2)
    outer(5, 1)
    parts = [mapped[i] for i in range(-1, count + 1)]
    forecast = cast_outer(outer_table(0), parts, *bands[0], model_noise, forecast)
    columns1 = [
        entry(pair1, 0, True, always), entry(long11, 1, longs, always), entry(short11, 1, shorts, ~end),
        entry(long12, 2, longs, always), entry(mixed4, 2, shorts, ~end), entry(long13, 3, longs, always),
        entry(over1, 1, shorts, end, 1 - y), entry(over2, 2, shorts, end, 1 - y), entry(last_over, 3, shorts, end, 1 - y),
    ]
    bands.append(place(columns1, part_flags(1)))
    half = 1 - y
    table = jnp.stack([half * part_blocks, half * (part_blocks // 2), (1 - y) * N, 2 * y * N]).astype(jnp.int32)
    return cast_rest(table, padded, parts, *bands[1], model_noise, forecast)


def solution(mesh):
    rows, cols = mesh.shape["row"], mesh.shape["col"]
    in_specs = (P("row", "col"), P("col", None, "row", None), P(), P("col", "row"))

    def step(covariance, blocks, present, model_noise):
        fits = rows == 8 and cols == 4 and blocks.shape[0] == 12 * cols
        chosen = body if fits and blocks.shape[3] == BS else plain_body
        inner = jax.shard_map(chosen, mesh=mesh, in_specs=in_specs, out_specs=P("col", "row"), check_vma=False)
        return inner(covariance, blocks, present, model_noise)

    return step
```

```python
import functools
import itertools

import jax
import jax.numpy as jnp
from jax import lax
from jax.experimental import pallas as pl
from jax.experimental.pallas import tpu as pltpu
from jax.sharding import PartitionSpec as P

F32 = jnp.float32
BF16 = jnp.bfloat16
BS = 256
MARGIN = 2 * BS
WIDE = 5 * BS
N = MARGIN
PLACED = 1
VMEM_BYTES = 56 * 2**20


def after(values, others):
    return lax.optimization_barrier((tuple(values), tuple(others)))[0]


def call(kernel, name, prefetch, grid, in_specs, out_specs, out_shape, scratch, args, flops, alias=None):
    moved = sum(a.size * a.dtype.itemsize for a in args) // 2
    return pl.pallas_call(
        kernel,
        grid_spec=pltpu.PrefetchScalarGridSpec(
            num_scalar_prefetch=len(prefetch), grid=grid, in_specs=in_specs, out_specs=out_specs, scratch_shapes=scratch
        ),
        out_shape=out_shape,
        input_output_aliases=alias or {},
        compiler_params=pltpu.CompilerParams(vmem_limit_bytes=VMEM_BYTES),
        cost_estimate=pl.CostEstimate(flops=flops, bytes_accessed=moved, transcendentals=0),
        name=name,
    )(*prefetch, *args)


def split_into(high_ref, low_ref, rows, value):
    high = value.astype(BF16)
    high_ref[rows, :] = high
    low_ref[rows, :] = (value - high.astype(F32)).astype(BF16)


def dot3(a_high, a_low, b_high, b_low):
    dot = functools.partial(jnp.dot, preferred_element_type=F32)
    return dot(a_high, b_high) + (dot(a_high, b_low) + dot(a_low, b_high))


def write_slabs(pieces, use, source, first, flags, block, high_ref, low_ref):
    slab = pieces[0].shape[3]
    for i, piece in enumerate(pieces):

        @pl.when(use[i] != 0)
        def _(i=i, piece=piece):
            for slot in range(2):
                side = first[i] if slot == 0 else 1 - first[i]
                rows = pl.ds(pl.multiple_of((source[i] * 2 + side) * slab, slab), slab)
                for d in range(5):
                    columns = pl.ds(d * BS, BS)
                    live = piece[slot, 0, d] * flags[block * 5 + d].astype(F32)
                    high = live.astype(BF16)
                    high_ref[rows, columns] = high
                    low_ref[rows, columns] = (live - high.astype(F32)).astype(BF16)


def slab_specs(pieces, row, at):
    def spec(i, piece, pair):
        return pl.BlockSpec((2, 1, 5, piece.shape[3], BS), lambda s, *tables: (pair, row(s) * tables[at][i], 0, 0, 0))

    return [spec(i, piece, pair) for i, (piece, pair) in enumerate(pieces)]


def place_kernel(count, use, source, first, flags, *refs):
    pieces, (high, low) = refs[:count], refs[count:]
    write_slabs(pieces, use, source, first, flags, pl.program_id(0), high.at[0], low.at[0])


def place(pieces, tables):
    blocks = pieces[0][0].shape[1]
    out = pl.BlockSpec((1, BS, WIDE), lambda b, *_: (b, 0, 0))
    return call(
        functools.partial(place_kernel, len(pieces)), "place_slabs", tables, (blocks,),
        slab_specs(pieces, lambda b: b, 0), [out] * 2,
        [jax.ShapeDtypeStruct((blocks, BS, WIDE), BF16)] * 2, [], [piece for piece, _ in pieces], 0,
    )


def place_last_kernel(count, use, source, first, flags, group, *refs):
    pieces, (high_before, low_before, high, low) = refs[:count], refs[count:]
    high[...] = high_before[...]
    low[...] = low_before[...]
    write_slabs(pieces, use, [0] * count, first, flags, pl.program_id(0), high.at[0], low.at[0])


def place_last(pieces, tables, high, low):
    blocks, _, slab = pieces[0][0].shape[1:4]
    group = pl.BlockSpec((1, 2 * slab, WIDE), lambda b, *t: (b, t[4][0], 0))
    return call(
        functools.partial(place_last_kernel, len(pieces)), "place_last", tables, (blocks,),
        slab_specs(pieces, lambda b: b, 0) + [group] * 2, [group] * 2,
        [jax.ShapeDtypeStruct(high.shape, BF16)] * 2, [], [piece for piece, _ in pieces] + [high, low], 0,
        {5 + len(pieces): 0, 6 + len(pieces): 1},
    )


def inner_kernel(count, y, own, *refs):
    nears, (high_a, low_a, high_b, low_b, out, head, tail, b_high, b_low) = refs[:count], refs[count:]
    step = pl.program_id(0)
    rows = own.shape[0]
    split_into(b_high, b_low, pl.ds(pl.multiple_of(y[0] * MARGIN, MARGIN), rows), own[...])
    at = pl.ds(pl.multiple_of((1 - y[0]) * rows, MARGIN), MARGIN)
    for i, near in enumerate(nears):

        @pl.when(step == i)
        def _(near=near):
            split_into(b_high, b_low, at, near[...])

    for j in range(4):
        high, low = (high_a, low_a) if j < 2 else (high_b, low_b)
        window = pl.ds(j * BS, WIDE)
        out[:, j * BS : (j + 1) * BS] = dot3(high[j % 2], low[j % 2], b_high[window, :], b_low[window, :]).T

    @pl.when(step == 0)
    def _():
        head[...] = out[...]

    @pl.when(step == count - 1)
    def _():
        tail[...] = out[...]


def map_inner(y, covariance, nears, row_high, row_low):
    rows, columns = covariance.shape
    pair_a = pl.BlockSpec((2, BS, WIDE), lambda s, y: (1 - y[0], 0, 0))
    pair_b = pl.BlockSpec((2, BS, WIDE), lambda s, y: (2 - y[0], 0, 0))
    edge = pl.BlockSpec((N, 4 * BS), lambda s, y: (0, 0))
    return call(
        functools.partial(inner_kernel, len(nears)), "map_inner", [y], (columns // N,),
        [pl.BlockSpec((rows, N), lambda s, y: (0, s))]
        + [pl.BlockSpec((MARGIN, N), lambda s, y, at=at: (0, at)) for _, at in nears]
        + [pair_a, pair_a, pair_b, pair_b],
        [pl.BlockSpec((N, 4 * BS), lambda s, y: (s, 0)), edge, edge],
        [jax.ShapeDtypeStruct((columns, 4 * BS), F32)] + [jax.ShapeDtypeStruct((N, 4 * BS), F32)] * 2,
        [pltpu.VMEM((rows + MARGIN, N), BF16)] * 2,
        [covariance, *[near for near, _ in nears], row_high, row_low, row_high, row_low], 6 * 4 * BS * WIDE * columns,
    )


def outer_kernel(count, y, chunks, own_a, own_b, *refs):
    fars, (high, low), outs, (b_high, b_low) = refs[:count], refs[count : count + 2], refs[count + 2 : -2], refs[-2:]
    at = lambda k: pl.ds(pl.multiple_of(k * MARGIN, MARGIN), MARGIN)
    split_into(b_high, b_low, at(1 - y[0]), own_a[...])
    split_into(b_high, b_low, at(2 - y[0]), own_b[...])
    for i, far in enumerate(fars):

        @pl.when(pl.program_id(0) == i)
        def _(far=far):
            split_into(b_high, b_low, at(2 * y[0]), far[...])

    for j in range(2):
        window = pl.ds(j * BS, WIDE)
        mapped = dot3(high[j], low[j], b_high[window, :], b_low[window, :]).T
        for i, out in enumerate(outs):

            @pl.when(pl.program_id(0) == i)
            def _(out=out):
                out[:, j * BS : (j + 1) * BS] = mapped


def map_outer(y, covariance, fars, row_high, row_low, chunks):
    pair = pl.BlockSpec((2, BS, WIDE), lambda s, y, c: (2 * y[0], 0, 0))
    return call(
        functools.partial(outer_kernel, len(fars)), "map_outer", [y, jnp.array(chunks, jnp.int32)], (len(chunks),),
        [
            pl.BlockSpec((MARGIN, N), lambda s, y, c: (y[0], c[s])),
            pl.BlockSpec((MARGIN, N), lambda s, y, c: (y[0] + 1, c[s])),
        ]
        + [pl.BlockSpec((MARGIN, N), lambda s, y, c, at=at: (0, at)) for _, at in fars]
        + [pair, pair],
        [pl.BlockSpec((N, 2 * BS), lambda s, y, c: (0, 0))] * len(chunks),
        [jax.ShapeDtypeStruct((N, 2 * BS), F32)] * len(chunks),
        [pltpu.VMEM((3 * MARGIN, N), BF16)] * 2,
        [covariance, covariance, *[far for far, _ in fars], row_high, row_low], 6 * 2 * BS * WIDE * N * len(chunks),
    )


def split_next(count, at, parts, high_ref, low_ref):
    rows = pl.ds(pl.multiple_of(pl.program_id(0) * BS, BS), BS)
    for part, here in zip(parts, (at < 2, (at >= 2) & (at < count + 2), at >= count + 2)):

        @pl.when(here)
        def _(part=part):
            split_into(high_ref, low_ref, rows, part[...])


def streams(count, width):
    def spec(first, blocks):
        return pl.BlockSpec((BS, width), lambda s, t, *_: (jnp.clip(t[0] + s - first, 0, blocks - 1), 0))

    return [spec(0, 2), spec(2, count), spec(count + 2, 2)]


def cast_inner_kernel(count, aliased, table, below, mid, above, high, low, noise, *rest):
    out, b_high, b_low = rest[aliased:]
    step = pl.program_id(0)
    split_next(count, table[0] + step, (below, mid, above), b_high, b_low)

    @pl.when(step >= 4)
    def _():
        window = pl.ds(pl.multiple_of((step - 4) * BS, BS), WIDE)
        out[...] = noise[...] + dot3(high[0], low[0], b_high[window, :], b_low[window, :])


def cast_inner(table, padded, high, low, noise, forecast):
    blocks, (length, width) = high.shape[0], padded[1].shape
    row = lambda s: jnp.maximum(s - 4, 0)
    place = pl.BlockSpec(
        (pl.Element(BS), pl.Element(width)), lambda s, t: (pl.multiple_of((t[0] + row(s)) * BS, BS), pl.multiple_of(t[1], N))
    )
    band = pl.BlockSpec((1, BS, WIDE), lambda s, t: (row(s), 0, 0))
    aliased = forecast is not None
    return call(
        functools.partial(cast_inner_kernel, length // BS, int(aliased)), "cast_inner", [table], (blocks + 4,),
        [*streams(length // BS, width), band, band, place]
        + [pl.BlockSpec(memory_space=pl.ANY)] * aliased,
        place, jax.ShapeDtypeStruct(noise.shape, F32), [pltpu.VMEM(((blocks + 4) * BS, width), BF16)] * 2,
        [*padded, high, low, noise] + [forecast] * aliased, 6 * blocks * BS * WIDE * width,
        {7: 0} if aliased else None,
    )


def cast_outer_kernel(count, held, table, *refs):
    parts, (high, low, noise, _, out, b_high, b_low) = refs[:count], refs[count:]
    step = pl.program_id(0)

    @pl.when(step == 0)
    def _():
        for i, part in enumerate(parts):

            @pl.when((i >= table[1]) & (i < table[1] + held))
            def _(i=i, part=part):
                split_into(b_high, b_low, pl.ds(pl.multiple_of((i - table[1]) * MARGIN, MARGIN), MARGIN), part[...])

    window = pl.ds(pl.multiple_of(step * BS, BS), WIDE)
    out[...] = noise[...] + dot3(high[0], low[0], b_high[window, :], b_low[window, :])


def cast_outer(table, parts, high, low, noise, forecast):
    blocks = high.shape[0]
    held = blocks // 2 + 2
    place = pl.BlockSpec((BS, N), lambda s, t: (t[0] + s, t[2]))
    band = pl.BlockSpec((1, BS, WIDE), lambda s, t: (s, 0, 0))
    return call(
        functools.partial(cast_outer_kernel, len(parts), held), "cast_outer", [table], (blocks,),
        [pl.BlockSpec((MARGIN, N), lambda s, t, at=at: (at, 0)) for _, at in parts]
        + [band, band, place, pl.BlockSpec(memory_space=pl.ANY)],
        place, jax.ShapeDtypeStruct(noise.shape, F32), [pltpu.VMEM((held * MARGIN, N), BF16)] * 2,
        [*[part for part, _ in parts], high, low, noise, forecast], 6 * blocks * BS * WIDE * N, {len(parts) + 4: 0},
    )


def cast_rest_kernel(length, count, held, slabs, table, use, source, first, flags, below, mid, above, *refs):
    parts, pieces, rest = refs[:count], refs[count : count + slabs], refs[count + slabs :]
    noise, _, out, in_high, in_low, out_high, out_low, high, low = rest
    step = pl.program_id(0)
    split_next(length, table[0] + step, (below, mid, above), in_high, in_low)

    @pl.when(step == 0)
    def _():
        for i, part in enumerate(parts):

            @pl.when((i >= table[1]) & (i < table[1] + held))
            def _(i=i, part=part):
                split_into(out_high, out_low, pl.ds(pl.multiple_of((i - table[1]) * MARGIN, MARGIN), MARGIN), part[...])

    @pl.when(step >= 4)
    def _():
        write_slabs(pieces, use, source, first, flags, step - 4, high, low)
        window = pl.ds(pl.multiple_of((step - 4) * BS, BS), WIDE)
        inner = pl.ds(pl.multiple_of(table[2], N), mid.shape[1])
        outer = pl.ds(pl.multiple_of(table[3], N), N)
        out[:, inner] = noise[:, inner] + dot3(high[...], low[...], in_high[window, :], in_low[window, :])
        out[:, outer] = noise[:, outer] + dot3(high[...], low[...], out_high[window, :], out_low[window, :])


def cast_rest(table, padded, parts, pieces, tables, noise, forecast):
    blocks, (length, width) = pieces[0][0].shape[1], padded[1].shape
    held = blocks // 2 + 2
    row = lambda s: jnp.maximum(s - 4, 0)
    place = pl.BlockSpec((BS, noise.shape[1]), lambda s, t, *_: (t[0] + row(s), 0))
    rows = (blocks + 4) * BS
    operands = [*padded, *[part for part, _ in parts], *[piece for piece, _ in pieces], noise, forecast]
    return call(
        functools.partial(cast_rest_kernel, length // BS, len(parts), held, len(pieces)), "cast_rest", [table, *tables],
        (blocks + 4,),
        streams(length // BS, width)
        + [pl.BlockSpec((MARGIN, N), lambda s, *_, at=at: (at, 0)) for _, at in parts]
        + slab_specs(pieces, row, 1)
        + [place, pl.BlockSpec(memory_space=pl.ANY)],
        place, jax.ShapeDtypeStruct(noise.shape, F32),
        [pltpu.VMEM((rows, width), BF16)] * 2 + [pltpu.VMEM((rows, N), BF16)] * 2 + [pltpu.VMEM((BS, WIDE), BF16)] * 2,
        operands, 6 * blocks * BS * WIDE * noise.shape[1], {5 + len(operands) - 1: 0},
    )


def spread(array, axis, root):
    mine = lax.axis_index(axis) == root
    return lax.psum(jnp.where(mine, array, jnp.zeros_like(array)), axis)


def padded_2(cells, sides, width):
    for axis, dim in sides:
        count = lax.axis_size(axis)
        ends = count - 1
        head = lax.slice_in_dim(cells, 0, width, axis=dim)
        tail = lax.slice_in_dim(cells, cells.shape[dim] - width, cells.shape[dim], axis=dim)
        cells = jnp.concatenate(
            [
                lax.ppermute(tail, axis, [(i, (i + 1) % count) for i in range(ends)]),
                cells,
                lax.ppermute(head, axis, [((i + 1) % count, i) for i in range(ends)]),
            ],
            axis=dim,
        )
    return cells


def band_apply(live_band, padded):
    blocks_here = live_band.shape[0]
    block_size = live_band.shape[2]
    columns = padded.shape[1]
    summed = None
    for diagonal in range(5):
        window = padded[diagonal * block_size : (diagonal + blocks_here) * block_size].reshape(
            blocks_here, block_size, columns
        )
        term = jnp.einsum(
            "bij,bjw->biw",
            live_band[:, diagonal],
            window,
            precision=lax.Precision.HIGHEST,
            preferred_element_type=jnp.float32,
        )
        summed = term if summed is None else summed + term
    return summed.reshape(blocks_here * block_size, columns)


def banded(live_band, field, halo_fn):
    return band_apply(live_band, halo_fn(field))


def plain_body(covariance, blocks, present, model_noise):
    row_index = lax.axis_index("row")
    col_index = lax.axis_index("col")
    ratio = lax.axis_size("row") // lax.axis_size("col")
    column_band = lax.all_gather(blocks, "row", axis=2, tiled=True)
    col_blocks = column_band.shape[0]
    row_blocks = col_blocks // ratio
    own_part = lax.dynamic_slice_in_dim(column_band, row_index % ratio * row_blocks, row_blocks, 0)
    row_band = spread(own_part, "col", row_index // ratio)
    flags = present.astype(jnp.float32)
    col_flags = lax.dynamic_slice_in_dim(flags, col_index * col_blocks, col_blocks, 0)
    row_flags = lax.dynamic_slice_in_dim(flags, row_index * row_blocks, row_blocks, 0)
    live_col = column_band * col_flags[:, :, None, None]
    live_row = row_band * row_flags[:, :, None, None]
    margin = 2 * blocks.shape[3]

    def row_margin(field):
        return padded_2(field, (("row", 0),), margin)

    def col_margin(field):
        return padded_2(field, (("col", 0),), margin)

    mapped = banded(live_row, covariance, row_margin)
    second = banded(live_col, mapped.T, col_margin)
    return second + model_noise


def body(covariance, blocks, present, model_noise):
    rows, cols = lax.axis_size("row"), lax.axis_size("col")
    r, c = lax.axis_index("row"), lax.axis_index("col")
    z, y = r // 2, r % 2
    depth = rows // 2
    col_blocks, _, slab, _ = blocks.shape
    part_blocks = col_blocks // 2
    swap = [(i, i ^ 1) for i in range(rows)]
    permute = lax.ppermute
    y_table = jnp.reshape(y, (1,)).astype(jnp.int32)

    sliced = blocks.reshape(2, part_blocks, 5, slab, BS)
    pick = lambda part: lax.dynamic_index_in_dim(sliced, part % 2, 0, False)

    def along(k, long, ends=True):
        hops = []
        for i in range(k - 1, depth - 1):
            hops.append((2 * i, 2 * i + 2) if long else (2 * i + 1, 2 * i + 3))
        for i in range(0, depth - k):
            hops.append((2 * i + 3, 2 * i + 1) if long else (2 * i + 2, 2 * i))
        return [(a, b) for a, b in hops if ends or b not in (0, rows - 1)]

    home = r // 2
    bits = [1 << b for b in reversed(range(cols.bit_length() - 1))]

    def senders(missing, bit, keep):
        pairs_of = [(i, a) for i in range(rows) if keep(i) for a in range(cols) if ((a ^ (i // 2)) & missing) == 0]
        return [(i * cols + a, i * cols + (a ^ bit)) for i, a in pairs_of]

    def keeps(k, long):
        def keep(i):
            up = (i % 2 == 0) == long
            return i // 2 >= k if up else i // 2 + k < depth

        return keep

    axes = ("row", "col")
    at_home, at_mate = c == home, c == home ^ bits[0]

    extra = covariance.shape[0] - MARGIN
    count = covariance.shape[1] // N
    chunks = sorted(range(count), key=lambda s: min(s, count - 1 - s))
    hops = [(i, i + 1) for i in range(1, rows - 1, 2)] + [(i + 1, i) for i in range(1, rows - 1, 2)]
    spans = [(0, 1), (1, 2), (3, 2), (5, 1)]
    near_trips = [
        (lax.dynamic_slice(covariance, (extra * (1 - y), at * N), (MARGIN, n * N)), "row", swap) for at, n in spans
    ]
    far_spans = [chunks[:1], chunks[1:3], chunks[3:5], chunks[5:]]
    far_trips = []
    for span in far_spans:
        pieces = [lax.dynamic_slice(covariance, (extra * y, i * N), (MARGIN, N)) for i in span]
        far_trips.append((jnp.concatenate(pieces, axis=1), "row", hops))

    def send(jobs, *others):
        values = after([job[0] for job in jobs], others)
        return [permute(value, axis, perm) for value, (_, axis, perm) in zip(values, jobs)]

    def pass_x(k, long):
        return senders(cols - 1, bits[0], keeps(k, long))

    def pass_core(k, long):
        return senders(cols - 1 - bits[0], bits[1], keeps(k, long))

    def join(*lists):
        return [pair for pairs in lists for pair in pairs]

    def whole(hops):
        return [(i * cols + a, j * cols + a) for i, j in hops for a in range(cols)]

    def among(hops):
        return functools.reduce(jnp.logical_or, [r == i for i, _ in hops])

    def core(value, passed, k, long):
        return permute(jnp.where(at_mate, passed, value), axes, pass_core(k, long))

    def climbed(k, up):
        return jnp.where(up, z >= k, z + k < depth), jnp.where(up, z - k, z + k)

    def entry(k, up, when, first=y):
        held, source = climbed(k, up)
        return held & when, jnp.clip(source, 0, depth - 1), first

    def either(k, when):
        above, below = entry(k, True, when), entry(k, False, when)
        return above[0] | below[0], jnp.where(z >= k, above[1], below[1]), y

    end = ((y == 0) & (z == 0)) | ((y == 1) & (z == depth - 1))
    always = z >= 0
    longs, shorts = y == 0, y == 1
    spots = (at_home, at_mate, ~(at_home | at_mate))

    def tables_of(entries, flags):
        return [jnp.stack([jnp.asarray(e[k], jnp.int32) for e in entries]) for k in range(3)] + [flags.reshape(-1)]

    def part_flags(phase):
        base = c * col_blocks + (y + phase) % 2 * part_blocks
        return lax.dynamic_slice_in_dim(present, base, part_blocks, 0)

    tables0 = tables_of(
        [entry(0, True, always), entry(1, longs, always), entry(1, shorts, always), either(2, always), either(3, always)],
        part_flags(0),
    )
    tables1 = tables_of(
        [
            entry(0, True, always), entry(1, longs, always), entry(1, shorts, ~end), entry(2, longs, always),
            entry(2, shorts, ~end), entry(3, longs, always), entry(1, shorts, end, 1 - y), entry(2, shorts, end, 1 - y),
            entry(3, shorts, end, 1 - y),
        ],
        part_flags(1),
    )
    row_flags = lax.dynamic_slice_in_dim(present, r * part_blocks, part_blocks, 0)
    row_tables = tables_of(
        [entry(0, True, spot) for spot in spots] + [entry(1, longs, spot) for spot in spots]
        + [entry(1, shorts, spot) for spot in spots] + [either(2, spot) for spot in spots], row_flags
    )
    last_tables = tables_of([either(3, spot) for spot in spots], row_flags)
    last_tables.append(jnp.reshape(either(3, always)[1], (1,)).astype(jnp.int32))
    half = 1 - y
    inner_table = jnp.stack([y * part_blocks, half * N]).astype(jnp.int32)
    outer_table = jnp.stack([y * part_blocks, y * (part_blocks // 2), 2 * y]).astype(jnp.int32)
    rest_table = jnp.stack([half * part_blocks, half * (part_blocks // 2), half * N, 2 * y * N]).astype(jnp.int32)
    all_tables = [*tables0, *tables1, *row_tables, *last_tables, inner_table, outer_table, rest_table, y_table]

    over = [(1, 0), (rows - 2, rows - 1)]
    ends_hops, inside_hops = along(3, False), along(1, False, False)
    trade0 = permute(pick(1 - y), "row", swap)
    pair0 = jnp.stack([pick(y), trade0])
    main = send(
        [(pick(1 - y + 1), "row", swap), near_trips[0], (pair0, "row", along(1, True)), (pair0, "row", along(1, False))], trade0
    )
    trade1, near0, long01, short01 = main
    (x0,) = send([(pair0, axes, pass_x(0, True))], trade1)
    pair1 = jnp.stack([pick(y + 1), trade1])
    stage = main + [x0] + [value for value, _, _ in near_trips[1:]] + all_tables
    main = send([near_trips[1], (long01, "row", along(2, True)), (short01, "row", along(2, False))], *stage)
    near1, long02, short02 = main
    x1a, core0 = send(
        [(long01, axes, pass_x(1, True)), (jnp.where(at_mate, x0, pair0), axes, pass_core(0, True))], *stage, pair1
    )
    climbs = lambda k: jnp.where(y == 0, z >= k, z + k < depth)
    stage = main + [x1a, core0] + [value for value, _, _ in far_trips]
    last_hops = along(3, True) + along(3, False)
    value2 = jnp.where(climbs(2), long02, short02)
    near2, ends3, short11, x2, x1b = main = send(
        [
            near_trips[2], (value2, "row", last_hops), (pair1, "row", along(1, False, False)),
            (value2, axes, senders(cols - 1, bits[0], lambda i: True)), (short01, axes, pass_x(1, False)),
        ],
        *stage,
    )
    (core1a,) = send([(jnp.where(at_mate, x1a, long01), axes, pass_core(1, True))], x2)
    stage = main + [core1a]
    inside2 = along(2, False, False)
    x3_keep = lambda i: i // 2 in (0, depth - 1)
    near3, far0, long11, mixed4, core12 = stage = send(
        [
            near_trips[3], far_trips[0], (pair1, "row", along(1, True)),
            (jnp.where(among(inside2), short11, ends3), axes, whole(inside2) + senders(cols - 1, bits[0], x3_keep)),
            (
                jnp.concatenate([jnp.where(at_mate, x1b, short01), jnp.where(at_mate, x2, value2)]),
                axes, senders(cols - 1 - bits[0], bits[1], lambda i: True),
            ),
        ],
        *stage,
    )

    plain = lambda *values: [value if isinstance(value, tuple) else (value, 0) for value in values]
    bands = [place(plain(pair0, long01, short01, value2, ends3), tables0)]
    core1b, core2 = (core12, 0), (core12, 1)
    row_parts = place(
        plain(pair0, x0, core0, long01, x1a, core1a, short01, x1b, core1b, value2, x2, core2), row_tables
    )
    stage = list(stage) + [bands[0][0], row_parts[0]]

    def outer(first, number):
        picked = list(range(first, first + number))
        outs = map_outer(y_table, covariance, [fars[i] for i in picked], row_high, row_low, [chunks[i] for i in picked])
        mapped.update((chunks[i], (out, 0)) for i, out in zip(picked, outs))
        return outs

    up, down = [(i, i + 1) for i in range(cols - 1)], [(i + 1, i) for i in range(cols - 1)]
    mapped, fars = {}, [(far0, 0)]
    stage4 = stage
    far12, long12, over1 = stage = send(
        [far_trips[1], (long11, "row", along(2, True)), (long01, "row", over)], *stage
    )
    (core3,) = send(
        [(jnp.where(at_mate, mixed4, ends3), axes, senders(cols - 1 - bits[0], bits[1], x3_keep))], *stage4
    )
    row_high, row_low = place_last(plain(ends3, mixed4, core3), last_tables, *row_parts)
    near_blocks = [(near, i) for near, (_, n) in zip((near0, near1, near2, near3), spans) for i in range(n)]
    inner, inner_head, inner_tail = map_inner(y_table, covariance, near_blocks, row_high, row_low)
    far34, long13, over2, below, above = stage = send(
        [
            far_trips[2], (long12, "row", along(3, True)), (long02, "row", over),
            (inner_tail, "col", up), (inner_head, "col", down),
        ],
        *stage, inner,
    )
    fars += [(far12, 0), (far12, 1), (far34, 0), (far34, 1)]
    first_mapped = outer(0, 3)
    padded = (below, inner, above)
    forecast = cast_inner(inner_table, padded, *bands[0], model_noise, None)
    far5, last_over, outer_below, outer_above = send(
        [far_trips[3], (ends3, "row", over), (mapped[count - 1][0], "col", up), (mapped[0][0], "col", down)],
        *stage, *first_mapped, forecast,
    )
    fars.append((far5, 0))
    mapped[-1], mapped[count] = (outer_below, 0), (outer_above, 0)
    outer(3, 2)
    outer(5, 1)
    parts = [mapped[i] for i in range(-1, count + 1)]
    forecast = cast_outer(outer_table, parts, *bands[0], model_noise, forecast)
    pieces1 = plain(pair1, long11, short11, long12, mixed4, long13, over1, over2, last_over)
    return cast_rest(rest_table, padded, parts, pieces1, tables1, model_noise, forecast)


def solution(mesh):
    rows, cols = mesh.shape["row"], mesh.shape["col"]
    in_specs = (P("row", "col"), P("col", None, "row", None), P(), P("col", "row"))

    def step(covariance, blocks, present, model_noise):
        fits = rows == 8 and cols == 4 and blocks.shape[0] == 12 * cols
        chosen = body if fits and blocks.shape[3] == BS else plain_body
        inner = jax.shard_map(chosen, mesh=mesh, in_specs=in_specs, out_specs=P("col", "row"), check_vma=False)
        return inner(covariance, blocks, present, model_noise)

    return step
```

```python
import functools
import itertools

import jax
import jax.numpy as jnp
from jax import lax
from jax.experimental import pallas as pl
from jax.experimental.pallas import tpu as pltpu
from jax.sharding import PartitionSpec as P

F32 = jnp.float32
BF16 = jnp.bfloat16
BS = 256
MARGIN = 2 * BS
WIDE = 5 * BS
N = MARGIN
PLACED = 1
VMEM_BYTES = 56 * 2**20


def after(values, others):
    return lax.optimization_barrier((tuple(values), tuple(others)))[0]


def call(kernel, name, prefetch, grid, in_specs, out_specs, out_shape, scratch, args, flops, alias=None):
    moved = sum(a.size * a.dtype.itemsize for a in args) // 2
    return pl.pallas_call(
        kernel,
        grid_spec=pltpu.PrefetchScalarGridSpec(
            num_scalar_prefetch=len(prefetch), grid=grid, in_specs=in_specs, out_specs=out_specs, scratch_shapes=scratch
        ),
        out_shape=out_shape,
        input_output_aliases=alias or {},
        compiler_params=pltpu.CompilerParams(vmem_limit_bytes=VMEM_BYTES),
        cost_estimate=pl.CostEstimate(flops=flops, bytes_accessed=moved, transcendentals=0),
        name=name,
    )(*prefetch, *args)


def split_into(high_ref, low_ref, rows, value):
    high = value.astype(BF16)
    high_ref[rows, :] = high
    low_ref[rows, :] = (value - high.astype(F32)).astype(BF16)


def dot3(a_high, a_low, b_high, b_low):
    dot = functools.partial(jnp.dot, preferred_element_type=F32)
    return dot(a_high, b_high) + (dot(a_high, b_low) + dot(a_low, b_high))


def write_slabs(pieces, use, source, first, flags, block, high_ref, low_ref):
    slab = pieces[0].shape[3]
    for i, piece in enumerate(pieces):

        @pl.when(use[i] != 0)
        def _(i=i, piece=piece):
            for slot in range(2):
                side = first[i] if slot == 0 else 1 - first[i]
                rows = pl.ds(pl.multiple_of((source[i] * 2 + side) * slab, slab), slab)
                for d in range(5):
                    columns = pl.ds(d * BS, BS)
                    live = piece[slot, 0, d] * flags[block * 5 + d].astype(F32)
                    high = live.astype(BF16)
                    high_ref[rows, columns] = high
                    low_ref[rows, columns] = (live - high.astype(F32)).astype(BF16)


def slab_specs(pieces, row, at):
    def spec(i, piece, pair):
        return pl.BlockSpec((2, 1, 5, piece.shape[3], BS), lambda s, *tables: (pair, row(s) * tables[at][i], 0, 0, 0))

    return [spec(i, piece, pair) for i, (piece, pair) in enumerate(pieces)]


def place_kernel(count, use, source, first, flags, *refs):
    pieces, (high, low) = refs[:count], refs[count:]
    write_slabs(pieces, use, source, first, flags, pl.program_id(0), high.at[0], low.at[0])


def place(pieces, tables):
    blocks = pieces[0][0].shape[1]
    out = pl.BlockSpec((1, BS, WIDE), lambda b, *_: (b, 0, 0))
    return call(
        functools.partial(place_kernel, len(pieces)), "place_slabs", tables, (blocks,),
        slab_specs(pieces, lambda b: b, 0), [out] * 2,
        [jax.ShapeDtypeStruct((blocks, BS, WIDE), BF16)] * 2, [], [piece for piece, _ in pieces], 0,
    )


def place_last_kernel(count, use, source, first, flags, group, *refs):
    pieces, (high_before, low_before, high, low) = refs[:count], refs[count:]
    high[...] = high_before[...]
    low[...] = low_before[...]
    write_slabs(pieces, use, [0] * count, first, flags, pl.program_id(0), high.at[0], low.at[0])


def place_last(pieces, tables, high, low):
    blocks, _, slab = pieces[0][0].shape[1:4]
    group = pl.BlockSpec((1, 2 * slab, WIDE), lambda b, *t: (b, t[4][0], 0))
    return call(
        functools.partial(place_last_kernel, len(pieces)), "place_last", tables, (blocks,),
        slab_specs(pieces, lambda b: b, 0) + [group] * 2, [group] * 2,
        [jax.ShapeDtypeStruct(high.shape, BF16)] * 2, [], [piece for piece, _ in pieces] + [high, low], 0,
        {5 + len(pieces): 0, 6 + len(pieces): 1},
    )


def inner_kernel(spans, y, own, *refs):
    count = len(spans)
    nears, (high_a, low_a, high_b, low_b, out, head, tail, b_high, b_low) = refs[:count], refs[count:]
    step = pl.program_id(0)
    rows = own.shape[0]
    split_into(b_high, b_low, pl.ds(pl.multiple_of(y[0] * MARGIN, MARGIN), rows), own[...])
    at = pl.ds(pl.multiple_of((1 - y[0]) * rows, MARGIN), MARGIN)
    for (at_step, n), near in zip(spans, nears):

        @pl.when((step >= at_step) & (step < at_step + n))
        def _(near=near):
            split_into(b_high, b_low, at, near[...])

    for j in range(4):
        high, low = (high_a, low_a) if j < 2 else (high_b, low_b)
        window = pl.ds(j * BS, WIDE)
        out[:, j * BS : (j + 1) * BS] = dot3(high[j % 2], low[j % 2], b_high[window, :], b_low[window, :]).T

    @pl.when(step == 0)
    def _():
        head[...] = out[...]

    @pl.when(step == pl.num_programs(0) - 1)
    def _():
        tail[...] = out[...]


def map_inner(y, covariance, nears, spans, row_high, row_low):
    rows, columns = covariance.shape
    pair_a = pl.BlockSpec((2, BS, WIDE), lambda s, y: (1 - y[0], 0, 0))
    pair_b = pl.BlockSpec((2, BS, WIDE), lambda s, y: (2 - y[0], 0, 0))
    edge = pl.BlockSpec((N, 4 * BS), lambda s, y: (0, 0))
    return call(
        functools.partial(inner_kernel, spans), "map_inner", [y], (columns // N,),
        [pl.BlockSpec((rows, N), lambda s, y: (0, s))]
        + [pl.BlockSpec((MARGIN, N), lambda s, y, at=at, n=n: (0, jnp.clip(s - at, 0, n - 1))) for at, n in spans]
        + [pair_a, pair_a, pair_b, pair_b],
        [pl.BlockSpec((N, 4 * BS), lambda s, y: (s, 0)), edge, edge],
        [jax.ShapeDtypeStruct((columns, 4 * BS), F32)] + [jax.ShapeDtypeStruct((N, 4 * BS), F32)] * 2,
        [pltpu.VMEM((rows + MARGIN, N), BF16)] * 2,
        [covariance, *nears, row_high, row_low, row_high, row_low], 6 * 4 * BS * WIDE * columns,
    )


def outer_kernel(count, y, chunks, own_a, own_b, *refs):
    fars, (high, low), outs, (b_high, b_low) = refs[:count], refs[count : count + 2], refs[count + 2 : -2], refs[-2:]
    at = lambda k: pl.ds(pl.multiple_of(k * MARGIN, MARGIN), MARGIN)
    split_into(b_high, b_low, at(1 - y[0]), own_a[...])
    split_into(b_high, b_low, at(2 - y[0]), own_b[...])
    for i, far in enumerate(fars):

        @pl.when(pl.program_id(0) == i)
        def _(far=far):
            split_into(b_high, b_low, at(2 * y[0]), far[...])

    for j in range(2):
        window = pl.ds(j * BS, WIDE)
        mapped = dot3(high[j], low[j], b_high[window, :], b_low[window, :]).T
        for i, out in enumerate(outs):

            @pl.when(pl.program_id(0) == i)
            def _(out=out):
                out[:, j * BS : (j + 1) * BS] = mapped


def map_outer(y, covariance, fars, row_high, row_low, chunks):
    pair = pl.BlockSpec((2, BS, WIDE), lambda s, y, c: (2 * y[0], 0, 0))
    return call(
        functools.partial(outer_kernel, len(fars)), "map_outer", [y, jnp.array(chunks, jnp.int32)], (len(chunks),),
        [
            pl.BlockSpec((MARGIN, N), lambda s, y, c: (y[0], c[s])),
            pl.BlockSpec((MARGIN, N), lambda s, y, c: (y[0] + 1, c[s])),
        ]
        + [pl.BlockSpec((MARGIN, N), lambda s, y, c, at=at: (0, at)) for _, at in fars]
        + [pair, pair],
        [pl.BlockSpec((N, 2 * BS), lambda s, y, c: (0, 0))] * len(chunks),
        [jax.ShapeDtypeStruct((N, 2 * BS), F32)] * len(chunks),
        [pltpu.VMEM((3 * MARGIN, N), BF16)] * 2,
        [covariance, covariance, *[far for far, _ in fars], row_high, row_low], 6 * 2 * BS * WIDE * N * len(chunks),
    )


def split_next(count, at, parts, high_ref, low_ref):
    rows = pl.ds(pl.multiple_of(pl.program_id(0) * BS, BS), BS)
    for part, here in zip(parts, (at < 2, (at >= 2) & (at < count + 2), at >= count + 2)):

        @pl.when(here)
        def _(part=part):
            split_into(high_ref, low_ref, rows, part[...])


def streams(count, width):
    def spec(first, blocks):
        return pl.BlockSpec((BS, width), lambda s, t, *_: (jnp.clip(t[0] + s - first, 0, blocks - 1), 0))

    return [spec(0, 2), spec(2, count), spec(count + 2, 2)]


def cast_inner_kernel(count, aliased, table, below, mid, above, high, low, noise, *rest):
    out, b_high, b_low = rest[aliased:]
    step = pl.program_id(0)
    split_next(count, table[0] + step, (below, mid, above), b_high, b_low)

    @pl.when(step >= 4)
    def _():
        window = pl.ds(pl.multiple_of((step - 4) * BS, BS), WIDE)
        out[...] = noise[...] + dot3(high[0], low[0], b_high[window, :], b_low[window, :])


def cast_inner(table, padded, high, low, noise, forecast):
    blocks, (length, width) = high.shape[0], padded[1].shape
    row = lambda s: jnp.maximum(s - 4, 0)
    place = pl.BlockSpec(
        (pl.Element(BS), pl.Element(width)), lambda s, t: (pl.multiple_of((t[0] + row(s)) * BS, BS), pl.multiple_of(t[1], N))
    )
    band = pl.BlockSpec((1, BS, WIDE), lambda s, t: (row(s), 0, 0))
    aliased = forecast is not None
    return call(
        functools.partial(cast_inner_kernel, length // BS, int(aliased)), "cast_inner", [table], (blocks + 4,),
        [*streams(length // BS, width), band, band, place]
        + [pl.BlockSpec(memory_space=pl.ANY)] * aliased,
        place, jax.ShapeDtypeStruct(noise.shape, F32), [pltpu.VMEM(((blocks + 4) * BS, width), BF16)] * 2,
        [*padded, high, low, noise] + [forecast] * aliased, 6 * blocks * BS * WIDE * width,
        {7: 0} if aliased else None,
    )


def cast_outer_kernel(count, held, table, *refs):
    parts, (high, low, noise, _, out, b_high, b_low) = refs[:count], refs[count:]
    step = pl.program_id(0)

    @pl.when(step == 0)
    def _():
        for i, part in enumerate(parts):

            @pl.when((i >= table[1]) & (i < table[1] + held))
            def _(i=i, part=part):
                split_into(b_high, b_low, pl.ds(pl.multiple_of((i - table[1]) * MARGIN, MARGIN), MARGIN), part[...])

    window = pl.ds(pl.multiple_of(step * BS, BS), WIDE)
    out[...] = noise[...] + dot3(high[0], low[0], b_high[window, :], b_low[window, :])


def cast_outer(table, parts, high, low, noise, forecast):
    blocks = high.shape[0]
    held = blocks // 2 + 2
    place = pl.BlockSpec((BS, N), lambda s, t: (t[0] + s, t[2]))
    band = pl.BlockSpec((1, BS, WIDE), lambda s, t: (s, 0, 0))
    return call(
        functools.partial(cast_outer_kernel, len(parts), held), "cast_outer", [table], (blocks,),
        [pl.BlockSpec((MARGIN, N), lambda s, t, at=at: (at, 0)) for _, at in parts]
        + [band, band, place, pl.BlockSpec(memory_space=pl.ANY)],
        place, jax.ShapeDtypeStruct(noise.shape, F32), [pltpu.VMEM((held * MARGIN, N), BF16)] * 2,
        [*[part for part, _ in parts], high, low, noise, forecast], 6 * blocks * BS * WIDE * N, {len(parts) + 4: 0},
    )


def cast_rest_kernel(length, count, held, slabs, table, use, source, first, flags, below, mid, above, *refs):
    parts, pieces, rest = refs[:count], refs[count : count + slabs], refs[count + slabs :]
    noise, _, out, in_high, in_low, out_high, out_low, high, low = rest
    step = pl.program_id(0)
    split_next(length, table[0] + step, (below, mid, above), in_high, in_low)

    @pl.when(step == 0)
    def _():
        for i, part in enumerate(parts):

            @pl.when((i >= table[1]) & (i < table[1] + held))
            def _(i=i, part=part):
                split_into(out_high, out_low, pl.ds(pl.multiple_of((i - table[1]) * MARGIN, MARGIN), MARGIN), part[...])

    @pl.when(step >= 4)
    def _():
        write_slabs(pieces, use, source, first, flags, step - 4, high, low)
        window = pl.ds(pl.multiple_of((step - 4) * BS, BS), WIDE)
        inner = pl.ds(pl.multiple_of(table[2], N), mid.shape[1])
        outer = pl.ds(pl.multiple_of(table[3], N), N)
        out[:, inner] = noise[:, inner] + dot3(high[...], low[...], in_high[window, :], in_low[window, :])
        out[:, outer] = noise[:, outer] + dot3(high[...], low[...], out_high[window, :], out_low[window, :])


def cast_rest(table, padded, parts, pieces, tables, noise, forecast):
    blocks, (length, width) = pieces[0][0].shape[1], padded[1].shape
    held = blocks // 2 + 2
    row = lambda s: jnp.maximum(s - 4, 0)
    place = pl.BlockSpec((BS, noise.shape[1]), lambda s, t, *_: (t[0] + row(s), 0))
    rows = (blocks + 4) * BS
    operands = [*padded, *[part for part, _ in parts], *[piece for piece, _ in pieces], noise, forecast]
    return call(
        functools.partial(cast_rest_kernel, length // BS, len(parts), held, len(pieces)), "cast_rest", [table, *tables],
        (blocks + 4,),
        streams(length // BS, width)
        + [pl.BlockSpec((MARGIN, N), lambda s, *_, at=at: (at, 0)) for _, at in parts]
        + slab_specs(pieces, row, 1)
        + [place, pl.BlockSpec(memory_space=pl.ANY)],
        place, jax.ShapeDtypeStruct(noise.shape, F32),
        [pltpu.VMEM((rows, width), BF16)] * 2 + [pltpu.VMEM((rows, N), BF16)] * 2 + [pltpu.VMEM((BS, WIDE), BF16)] * 2,
        operands, 6 * blocks * BS * WIDE * noise.shape[1], {5 + len(operands) - 1: 0},
    )


def spread(array, axis, root):
    mine = lax.axis_index(axis) == root
    return lax.psum(jnp.where(mine, array, jnp.zeros_like(array)), axis)


def padded_2(cells, sides, width):
    for axis, dim in sides:
        count = lax.axis_size(axis)
        ends = count - 1
        head = lax.slice_in_dim(cells, 0, width, axis=dim)
        tail = lax.slice_in_dim(cells, cells.shape[dim] - width, cells.shape[dim], axis=dim)
        cells = jnp.concatenate(
            [
                lax.ppermute(tail, axis, [(i, (i + 1) % count) for i in range(ends)]),
                cells,
                lax.ppermute(head, axis, [((i + 1) % count, i) for i in range(ends)]),
            ],
            axis=dim,
        )
    return cells


def band_apply(live_band, padded):
    blocks_here = live_band.shape[0]
    block_size = live_band.shape[2]
    columns = padded.shape[1]
    summed = None
    for diagonal in range(5):
        window = padded[diagonal * block_size : (diagonal + blocks_here) * block_size].reshape(
            blocks_here, block_size, columns
        )
        term = jnp.einsum(
            "bij,bjw->biw",
            live_band[:, diagonal],
            window,
            precision=lax.Precision.HIGHEST,
            preferred_element_type=jnp.float32,
        )
        summed = term if summed is None else summed + term
    return summed.reshape(blocks_here * block_size, columns)


def banded(live_band, field, halo_fn):
    return band_apply(live_band, halo_fn(field))


def plain_body(covariance, blocks, present, model_noise):
    row_index = lax.axis_index("row")
    col_index = lax.axis_index("col")
    ratio = lax.axis_size("row") // lax.axis_size("col")
    column_band = lax.all_gather(blocks, "row", axis=2, tiled=True)
    col_blocks = column_band.shape[0]
    row_blocks = col_blocks // ratio
    own_part = lax.dynamic_slice_in_dim(column_band, row_index % ratio * row_blocks, row_blocks, 0)
    row_band = spread(own_part, "col", row_index // ratio)
    flags = present.astype(jnp.float32)
    col_flags = lax.dynamic_slice_in_dim(flags, col_index * col_blocks, col_blocks, 0)
    row_flags = lax.dynamic_slice_in_dim(flags, row_index * row_blocks, row_blocks, 0)
    live_col = column_band * col_flags[:, :, None, None]
    live_row = row_band * row_flags[:, :, None, None]
    margin = 2 * blocks.shape[3]

    def row_margin(field):
        return padded_2(field, (("row", 0),), margin)

    def col_margin(field):
        return padded_2(field, (("col", 0),), margin)

    mapped = banded(live_row, covariance, row_margin)
    second = banded(live_col, mapped.T, col_margin)
    return second + model_noise


def body(covariance, blocks, present, model_noise):
    rows, cols = lax.axis_size("row"), lax.axis_size("col")
    r, c = lax.axis_index("row"), lax.axis_index("col")
    z, y = r // 2, r % 2
    depth = rows // 2
    col_blocks, _, slab, _ = blocks.shape
    part_blocks = col_blocks // 2
    swap = [(i, i ^ 1) for i in range(rows)]
    permute = lax.ppermute
    y_table = jnp.reshape(y, (1,)).astype(jnp.int32)

    sliced = blocks.reshape(2, part_blocks, 5, slab, BS)
    pick = lambda part: lax.dynamic_index_in_dim(sliced, part % 2, 0, False)

    def along(k, long, ends=True):
        hops = []
        for i in range(k - 1, depth - 1):
            hops.append((2 * i, 2 * i + 2) if long else (2 * i + 1, 2 * i + 3))
        for i in range(0, depth - k):
            hops.append((2 * i + 3, 2 * i + 1) if long else (2 * i + 2, 2 * i))
        return [(a, b) for a, b in hops if ends or b not in (0, rows - 1)]

    home = r // 2
    bits = [1 << b for b in reversed(range(cols.bit_length() - 1))]

    def senders(missing, bit, keep):
        pairs_of = [(i, a) for i in range(rows) if keep(i) for a in range(cols) if ((a ^ (i // 2)) & missing) == 0]
        return [(i * cols + a, i * cols + (a ^ bit)) for i, a in pairs_of]

    def keeps(k, long):
        def keep(i):
            up = (i % 2 == 0) == long
            return i // 2 >= k if up else i // 2 + k < depth

        return keep

    axes = ("row", "col")
    at_home, at_mate = c == home, c == home ^ bits[0]

    extra = covariance.shape[0] - MARGIN
    count = covariance.shape[1] // N
    chunks = sorted(range(count), key=lambda s: min(s, count - 1 - s))
    hops = [(i, i + 1) for i in range(1, rows - 1, 2)] + [(i + 1, i) for i in range(1, rows - 1, 2)]
    spans = [(0, 1), (1, 2), (3, 2), (5, 1)]
    near_trips = [
        (lax.dynamic_slice(covariance, (extra * (1 - y), at * N), (MARGIN, n * N)), "row", swap) for at, n in spans
    ]
    far_spans = [chunks[:1], chunks[1:3], chunks[3:5], chunks[5:]]
    far_trips = []
    for span in far_spans:
        pieces = [lax.dynamic_slice(covariance, (extra * y, i * N), (MARGIN, N)) for i in span]
        far_trips.append((jnp.concatenate(pieces, axis=1), "row", hops))

    def send(jobs, *others):
        values = after([job[0] for job in jobs], others)
        return [permute(value, axis, perm) for value, (_, axis, perm) in zip(values, jobs)]

    def pass_x(k, long):
        return senders(cols - 1, bits[0], keeps(k, long))

    def pass_core(k, long):
        return senders(cols - 1 - bits[0], bits[1], keeps(k, long))

    def join(*lists):
        return [pair for pairs in lists for pair in pairs]

    def whole(hops):
        return [(i * cols + a, j * cols + a) for i, j in hops for a in range(cols)]

    def among(hops):
        return functools.reduce(jnp.logical_or, [r == i for i, _ in hops])

    def core(value, passed, k, long):
        return permute(jnp.where(at_mate, passed, value), axes, pass_core(k, long))

    def climbed(k, up):
        return jnp.where(up, z >= k, z + k < depth), jnp.where(up, z - k, z + k)

    def entry(k, up, when, first=y):
        held, source = climbed(k, up)
        return held & when, jnp.clip(source, 0, depth - 1), first

    def either(k, when):
        above, below = entry(k, True, when), entry(k, False, when)
        return above[0] | below[0], jnp.where(z >= k, above[1], below[1]), y

    end = ((y == 0) & (z == 0)) | ((y == 1) & (z == depth - 1))
    always = z >= 0
    longs, shorts = y == 0, y == 1
    spots = (at_home, at_mate, ~(at_home | at_mate))

    def tables_of(entries, flags):
        return [jnp.stack([jnp.asarray(e[k], jnp.int32) for e in entries]) for k in range(3)] + [flags.reshape(-1)]

    def part_flags(phase):
        base = c * col_blocks + (y + phase) % 2 * part_blocks
        return lax.dynamic_slice_in_dim(present, base, part_blocks, 0)

    tables0 = tables_of(
        [entry(0, True, always), entry(1, longs, always), entry(1, shorts, always), either(2, always), either(3, always)],
        part_flags(0),
    )
    tables1 = tables_of(
        [
            entry(0, True, always), entry(1, longs, always), entry(1, shorts, ~end), entry(2, longs, always),
            entry(2, shorts, ~end), entry(3, longs, always), entry(1, shorts, end, 1 - y), entry(2, shorts, end, 1 - y),
            entry(3, shorts, end, 1 - y),
        ],
        part_flags(1),
    )
    row_flags = lax.dynamic_slice_in_dim(present, r * part_blocks, part_blocks, 0)
    row_tables = tables_of(
        [entry(0, True, spot) for spot in spots] + [entry(1, longs, spot) for spot in spots]
        + [entry(1, shorts, spot) for spot in spots] + [either(2, spot) for spot in spots], row_flags
    )
    last_tables = tables_of([either(3, spot) for spot in spots], row_flags)
    last_tables.append(jnp.reshape(either(3, always)[1], (1,)).astype(jnp.int32))
    half = 1 - y
    inner_table = jnp.stack([y * part_blocks, half * N]).astype(jnp.int32)
    outer_table = jnp.stack([y * part_blocks, y * (part_blocks // 2), 2 * y]).astype(jnp.int32)
    rest_table = jnp.stack([half * part_blocks, half * (part_blocks // 2), half * N, 2 * y * N]).astype(jnp.int32)
    all_tables = [*tables0, *tables1, *row_tables, *last_tables, inner_table, outer_table, rest_table, y_table]

    over = [(1, 0), (rows - 2, rows - 1)]
    ends_hops, inside_hops = along(3, False), along(1, False, False)
    trade0 = permute(pick(1 - y), "row", swap)
    pair0 = jnp.stack([pick(y), trade0])
    main = send(
        [(pick(1 - y + 1), "row", swap), near_trips[0], (pair0, "row", along(1, True)), (pair0, "row", along(1, False))], trade0
    )
    trade1, near0, long01, short01 = main
    (x0,) = send([(pair0, axes, pass_x(0, True))], trade1)
    pair1 = jnp.stack([pick(y + 1), trade1])
    stage = main + [x0] + [value for value, _, _ in near_trips[1:]] + all_tables
    main = send([near_trips[1], (long01, "row", along(2, True)), (short01, "row", along(2, False))], *stage)
    near1, long02, short02 = main
    x1a, core0 = send(
        [(long01, axes, pass_x(1, True)), (jnp.where(at_mate, x0, pair0), axes, pass_core(0, True))], *stage, pair1
    )
    climbs = lambda k: jnp.where(y == 0, z >= k, z + k < depth)
    stage = main + [x1a, core0] + [value for value, _, _ in far_trips]
    last_hops = along(3, True) + along(3, False)
    value2 = jnp.where(climbs(2), long02, short02)
    near2, short11 = main = send([near_trips[2], (pair1, "row", along(1, False, False))], *stage)
    ends3, x2, x1b = rest = send(
        [
            (value2, "row", last_hops), (value2, axes, senders(cols - 1, bits[0], lambda i: True)),
            (short01, axes, pass_x(1, False)),
        ],
        *stage,
    )
    main = main + rest
    (core1a,) = send([(jnp.where(at_mate, x1a, long01), axes, pass_core(1, True))], x2)
    stage = main + [core1a]
    inside2 = along(2, False, False)
    x3_keep = lambda i: i // 2 in (0, depth - 1)
    near3, far0, long11, mixed4, core12 = stage = send(
        [
            near_trips[3], far_trips[0], (pair1, "row", along(1, True)),
            (jnp.where(among(inside2), short11, ends3), axes, whole(inside2) + senders(cols - 1, bits[0], x3_keep)),
            (
                jnp.concatenate([jnp.where(at_mate, x1b, short01), jnp.where(at_mate, x2, value2)]),
                axes, senders(cols - 1 - bits[0], bits[1], lambda i: True),
            ),
        ],
        *stage,
    )

    plain = lambda *values: [value if isinstance(value, tuple) else (value, 0) for value in values]
    bands = [place(plain(pair0, long01, short01, value2, ends3), tables0)]
    core1b, core2 = (core12, 0), (core12, 1)
    row_parts = place(
        plain(pair0, x0, core0, long01, x1a, core1a, short01, x1b, core1b, value2, x2, core2), row_tables
    )
    stage = list(stage) + [bands[0][0], row_parts[0]]

    def outer(first, number):
        picked = list(range(first, first + number))
        outs = map_outer(y_table, covariance, [fars[i] for i in picked], row_high, row_low, [chunks[i] for i in picked])
        mapped.update((chunks[i], (out, 0)) for i, out in zip(picked, outs))
        return outs

    up, down = [(i, i + 1) for i in range(cols - 1)], [(i + 1, i) for i in range(cols - 1)]
    mapped, fars = {}, [(far0, 0)]
    stage4 = stage
    far12, long12, over1 = stage = send(
        [far_trips[1], (long11, "row", along(2, True)), (long01, "row", over)], *stage
    )
    (core3,) = send(
        [(jnp.where(at_mate, mixed4, ends3), axes, senders(cols - 1 - bits[0], bits[1], x3_keep))], *stage4
    )
    row_high, row_low = place_last(plain(ends3, mixed4, core3), last_tables, *row_parts)
    inner, inner_head, inner_tail = map_inner(y_table, covariance, [near0, near1, near2, near3], spans, row_high, row_low)
    far34, long13, over2, below, above = stage = send(
        [
            far_trips[2], (long12, "row", along(3, True)), (long02, "row", over),
            (inner_tail, "col", up), (inner_head, "col", down),
        ],
        *stage, inner,
    )
    fars += [(far12, 0), (far12, 1), (far34, 0), (far34, 1)]
    first_mapped = outer(0, 3)
    padded = (below, inner, above)
    forecast = cast_inner(inner_table, padded, *bands[0], model_noise, None)
    far5, last_over, outer_below, outer_above = send(
        [far_trips[3], (ends3, "row", over), (mapped[count - 1][0], "col", up), (mapped[0][0], "col", down)],
        *stage, *first_mapped, forecast,
    )
    fars.append((far5, 0))
    mapped[-1], mapped[count] = (outer_below, 0), (outer_above, 0)
    outer(3, 2)
    outer(5, 1)
    parts = [mapped[i] for i in range(-1, count + 1)]
    forecast = cast_outer(outer_table, parts, *bands[0], model_noise, forecast)
    pieces1 = plain(pair1, long11, short11, long12, mixed4, long13, over1, over2, last_over)
    return cast_rest(rest_table, padded, parts, pieces1, tables1, model_noise, forecast)


def solution(mesh):
    rows, cols = mesh.shape["row"], mesh.shape["col"]
    in_specs = (P("row", "col"), P("col", None, "row", None), P(), P("col", "row"))

    def step(covariance, blocks, present, model_noise):
        fits = rows == 8 and cols == 4 and blocks.shape[0] == 12 * cols
        chosen = body if fits and blocks.shape[3] == BS else plain_body
        inner = jax.shard_map(chosen, mesh=mesh, in_specs=in_specs, out_specs=P("col", "row"), check_vma=False)
        return inner(covariance, blocks, present, model_noise)

    return step
```
